32 devices in a mesh: groups: 2 (over y), replica: 4 (over x, core), tensor: 4 (over z).
Axes of the slice: x: 2, y: 2, z: 4, core: 2. Of those that a mesh axis runs over, the one named last changes fastest.
Arguments:
- layer_input: bfloat16 [6144, 8192], P(('groups', 'replica', 'tensor')), parts along dimension 0, may hold values from -6 to 6
- input_norm_weight: bfloat16 [8192], replicated, may hold values from 0.099609375 to 1.8984375
- query_base_matrix: bfloat16 [8192, 8192], P(None, 'tensor'), may hold values from -0.0625 to 0.0625
- adapter_down_weight: bfloat16 [4, 8192, 64], P('replica'), may hold values from -0.0625 to 0.0625
- adapter_up_weight: bfloat16 [4, 64, 8192], P('replica', None, 'tensor'), may hold values from -0.75 to 0.75
- token_adapter_index: int32 [6144], P(('groups', 'replica')), parts along dimension 0, may hold values from 0 to 3
Outputs:
- queries: bfloat16 [6144, 8192], P(('groups', 'replica'), 'tensor'), parts along dimension 0
The draws below stay inside these ranges and needn't reach their ends.
There are 2 independent parts, one for each index of `groups`. The reference program is written for one: setup_inputs(seed, part) draws one part's arguments, and reference() takes and returns one part's arrays. A program takes and returns all parts, laid end to end along the dimension named above; an argument that names none is the same for every part. Nothing has to cross between parts.
All inputs are finite; a program needn't handle non-finite values.
Results may differ from the reference program's by a relative error of at most 0.0055.
Values may be sent and summed in bfloat16 or wider, within the bound.
No kernel may reach another device: no remote copies, remote signals or barrier semaphores. Data moves between devices by JAX's collectives and lax.ppermute only.
A program may use at most 128 MiB of HBM per device.

```python
import math
import jax
import jax.numpy as jnp
import numpy as np
from jax import lax

MODEL_WIDTH = 8192
ADAPTER_RANK = 64
QUERY_FEATURES = 8192
ADAPTER_POOL = 4
TOKENS = 3072


def plant(entries, own_key, least, top_value):
    extent = entries.shape
    index_at = [jax.random.randint(jax.random.fold_in(own_key, axis), (), 0, extent[axis]) for axis in range(len(extent))]
    entries = entries.at[tuple(index_at)].set(least)
    longest = extent.index(max(extent))
    index_at[longest] = (index_at[longest] + 1) % extent[longest]
    return entries.at[tuple(index_at)].set(top_value)


def block_levels(key, shape, pieces, smallest, largest):
    gain = 1.0
    for dim, shards_of in pieces:
        draws = jax.random.uniform(jax.random.fold_in(jax.random.fold_in(key, 6), dim), (shards_of,), jnp.float32, smallest / len(pieces), largest / len(pieces))
        gain = gain * jnp.repeat(jnp.exp(draws), shape[dim] // shards_of).reshape((-1,) + (1,) * (len(shape) - 1 - dim))
    return gain


def cumulative_ranks(amount, lean):
    weights = [(1 << 20) // math.isqrt(standing ** lean) + 1 for standing in range(1, amount + 1)]
    width = 1 + sum(weights) // (1 << 30)
    return np.cumsum(np.array([max(1, weight // width) for weight in weights]))


def ranked_ids(rng, extent, amount, skew):
    grid = cumulative_ranks(amount, skew)
    pick = jax.random.randint(jax.random.fold_in(rng, 1), extent, 0, int(grid[amount - 1]))
    rank = jnp.searchsorted(jnp.asarray(grid, jnp.int32), pick, side="right")
    return jax.random.permutation(jax.random.fold_in(rng, 2), amount)[rank].astype(jnp.int32)


def gaussian(stream_key, extent, deviation, bound, cuts=(), kind=jnp.bfloat16):
    entries = jax.random.normal(stream_key, extent, jnp.float32) * deviation
    if len(cuts) > 0:
        entries = block_levels(stream_key, extent, cuts, -0.22, 0.18) * entries
    return jnp.clip(entries, min=-bound, max=bound).astype(kind)


def setup_inputs(seed: int = 0, part: int = 0) -> dict:
    key_of = jax.random.split(jax.random.key(seed), 7)
    part_keys = jax.random.split(jax.random.fold_in(key_of[6], part), 7)
    layer_input = gaussian(part_keys[0], (TOKENS, MODEL_WIDTH), 1.0, 6.0, ((0, 16),))
    input_norm_weight = jnp.clip(1.0 + 0.18 * jax.random.normal(key_of[1], (MODEL_WIDTH,), jnp.float32), 0.099609375, 1.8984375).astype(jnp.bfloat16)
    query_base_matrix = gaussian(key_of[2], (MODEL_WIDTH, QUERY_FEATURES), MODEL_WIDTH ** -0.5, 0.0625, ((1, 4),))
    adapter_down_weight = gaussian(key_of[3], (ADAPTER_POOL, MODEL_WIDTH, ADAPTER_RANK), MODEL_WIDTH ** -0.5, 0.0625, ((0, 4),))
    adapter_up_weight = gaussian(key_of[4], (ADAPTER_POOL, ADAPTER_RANK, QUERY_FEATURES), ADAPTER_RANK ** -0.5, 0.75, ((0, 4), (2, 4)))
    token_adapter_index = plant(ranked_ids(part_keys[5], (TOKENS,), ADAPTER_POOL, 2), jax.random.fold_in(part_keys[5], 3), 0, ADAPTER_POOL - 1).astype(jnp.int32)
    return {"layer_input": layer_input, "input_norm_weight": input_norm_weight, "query_base_matrix": query_base_matrix, "adapter_down_weight": adapter_down_weight, "adapter_up_weight": adapter_up_weight, "token_adapter_index": token_adapter_index}


adapter_scale = 2.0

def reference(layer_input, input_norm_weight, query_base_matrix, adapter_down_weight, adapter_up_weight, token_adapter_index):
    xf = layer_input.astype(jnp.float32)
    ms = lax.optimization_barrier(jnp.mean(xf * xf, axis=-1, keepdims=True))
    normed = (xf * lax.rsqrt(ms + 1e-05) * input_norm_weight.astype(jnp.float32)).astype(jnp.bfloat16)
    adapter_count = adapter_down_weight.shape[0]
    onehot = (token_adapter_index[:, None] == jnp.arange(adapter_count, dtype=jnp.int32)[None, :]).astype(jnp.float32)
    flattened_down = jnp.transpose(adapter_down_weight, (1, 0, 2)).reshape(MODEL_WIDTH, adapter_count * ADAPTER_RANK)
    low_all = jnp.dot(normed, flattened_down, preferred_element_type=jnp.float32).reshape(-1, adapter_count, ADAPTER_RANK)
    low = lax.optimization_barrier(jnp.sum(onehot[:, :, None] * low_all, axis=1)).astype(jnp.bfloat16)
    masked_update = (onehot[:, :, None] * low[:, None, :].astype(jnp.float32)).reshape(-1, adapter_count * ADAPTER_RANK).astype(jnp.bfloat16)
    adapter_update = jnp.dot(masked_update, adapter_up_weight.reshape(adapter_count * ADAPTER_RANK, QUERY_FEATURES), preferred_element_type=jnp.float32)
    base_output = jnp.dot(normed, query_base_matrix, preferred_element_type=jnp.float32)
    return (base_output + adapter_scale * adapter_update).astype(jnp.bfloat16)
```

```python
import jax
import jax.numpy as jnp
from jax import lax
from jax.sharding import PartitionSpec as P

adapter_scale = 2.0


def body(
    layer_input,
    input_norm_weight,
    query_base_matrix,
    adapter_down_weight,
    adapter_up_weight,
    token_adapter_index,
):
    xf = layer_input.astype(jnp.float32)
    ms = jnp.mean(xf * xf, axis=-1, keepdims=True)
    normed = (xf * lax.rsqrt(ms + 1e-05) * input_norm_weight.astype(jnp.float32)).astype(
        jnp.bfloat16
    )
    width = layer_input.shape[1]
    parts = 4
    step = width // parts
    gathered = [
        lax.all_gather(normed[:, i * step : (i + 1) * step], "tensor", axis=0, tiled=True)
        for i in range(parts)
    ]
    count = lax.axis_size("replica")
    me = lax.axis_index("replica")
    down, up = [adapter_down_weight[0]], [adapter_up_weight[0]]
    for hop in range(1, count):
        pairs = [(i, i ^ hop if count == 4 else (i + hop) % count) for i in range(count)]
        down.append(lax.ppermute(adapter_down_weight[0], "replica", pairs))
        up.append(lax.ppermute(adapter_up_weight[0], "replica", pairs))
    if count == 4:
        owners = [me ^ hop for hop in range(count)]
    else:
        owners = [(me - hop) % count for hop in range(count)]
    down_cat = jnp.concatenate(down, axis=1)
    up_cat = jnp.concatenate(up, axis=0)
    rank = adapter_down_weight.shape[2]
    total = low_all = None
    for i in range(parts):
        rows = slice(i * step, (i + 1) * step)
        p = jnp.dot(gathered[i], query_base_matrix[rows], preferred_element_type=jnp.float32)
        q = jnp.dot(gathered[i], down_cat[rows], preferred_element_type=jnp.float32)
        total = p if total is None else total + p
        low_all = q if low_all is None else low_all + q
    column_owner = jnp.repeat(jnp.stack(owners), rank).astype(jnp.int32)
    chosen = token_adapter_index[:, None] == column_owner[None, :]
    masked = jnp.where(chosen, low_all, 0.0).astype(jnp.bfloat16)
    update = jnp.dot(masked, up_cat, preferred_element_type=jnp.float32)
    return (total + adapter_scale * update).astype(jnp.bfloat16)


def solution(mesh):
    placed = (
        P(("groups", "replica", "tensor"), None),
        P(),
        P(None, "tensor"),
        P("replica", None, None),
        P("replica", None, "tensor"),
        P(("groups", "replica")),
    )
    return jax.shard_map(
        body,
        mesh=mesh,
        in_specs=placed,
        out_specs=P(("groups", "replica"), "tensor"),
        check_vma=False,
    )
```

```python
import jax
import jax.numpy as jnp
from jax import lax
from jax.experimental import pallas as pl
from jax.experimental.pallas import tpu as pltpu
from jax.sharding import PartitionSpec as P

adapter_scale = 2.0
lanes = 128
vmem = 56 * 1024 * 1024
f32 = jnp.float32
bf16 = jnp.bfloat16


def plain(
    layer_input,
    input_norm_weight,
    query_base_matrix,
    adapter_down_weight,
    adapter_up_weight,
    token_adapter_index,
):
    xf = layer_input.astype(f32)
    ms = jnp.mean(xf * xf, axis=-1, keepdims=True)
    normed = (xf * lax.rsqrt(ms + 1e-05) * input_norm_weight.astype(f32)).astype(bf16)
    gathered = lax.all_gather(normed, "tensor", axis=0, tiled=True)
    down_all = lax.all_gather(adapter_down_weight, "replica", axis=0, tiled=True)
    up_all = lax.all_gather(adapter_up_weight, "replica", axis=0, tiled=True)
    count, width, rank = down_all.shape
    down_cat = jnp.transpose(down_all, (1, 0, 2)).reshape(width, count * rank)
    low_all = jnp.dot(gathered, down_cat, preferred_element_type=f32)
    owner = jnp.repeat(jnp.arange(count, dtype=jnp.int32), rank)
    chosen = token_adapter_index[:, None] == owner[None, :]
    masked = jnp.where(chosen, low_all, 0.0).astype(bf16)
    update = jnp.dot(
        masked, up_all.reshape(count * rank, up_all.shape[2]), preferred_element_type=f32
    )
    base = jnp.dot(gathered, query_base_matrix, preferred_element_type=f32)
    return (base + adapter_scale * update).astype(bf16)


def norm_chunks(x, gain, parts):
    rows, width = x.shape
    step = width // parts
    block = 48

    def kernel(x_ref, g_ref, *out_refs):
        xf = x_ref[...].astype(f32)
        ms = jnp.mean(xf * xf, axis=-1, keepdims=True)
        y = (xf * lax.rsqrt(ms + 1e-05) * g_ref[...].astype(f32)).astype(bf16)
        for i, out_ref in enumerate(out_refs):
            out_ref[...] = y[:, i * step : (i + 1) * step]

    return pl.pallas_call(
        kernel,
        grid=(rows // block,),
        in_specs=[
            pl.BlockSpec((block, width), lambda i: (i, 0)),
            pl.BlockSpec((1, width), lambda i: (0, 0)),
        ],
        out_specs=[pl.BlockSpec((block, step), lambda i: (i, 0))] * parts,
        out_shape=[jax.ShapeDtypeStruct((rows, step), bf16)] * parts,
        compiler_params=pltpu.CompilerParams(vmem_limit_bytes=vmem),
        cost_estimate=pl.CostEstimate(
            flops=5 * rows * width, bytes_accessed=4 * rows * width, transcendentals=rows
        ),
        name="norm_chunks",
    )(x, gain)


def dot_t(a, b):
    return lax.dot_general(a, b, (((1,), (1,)), ((), ())), preferred_element_type=f32)


def product(first, xs, weight, pool, carry=None, finish=None):
    rows, step = xs[0][0].shape
    width, features = weight.shape
    pool_rows = pool.shape[0]
    tile = 512
    tiles = features // tile
    steps = len(xs)
    flat = [a for t in xs for a in t]
    has_partial = finish is not None and finish["partial"] is not None
    has_prev = finish is not None and finish["prev"] is not None

    def kernel(row_ref, *refs):
        refs = list(refs)
        x_refs = [refs.pop(0) for _ in flat]
        w_ref, down_ref = refs.pop(0), refs.pop(0)
        acc_in = low_in = None
        if carry is not None:
            acc_in, low_in = refs.pop(0), refs.pop(0)
        if finish is not None:
            up_ref, owner_ref, ids_ref = refs.pop(0), refs.pop(0), refs.pop(0)
            part_ref = refs.pop(0) if has_partial else None
            if has_prev:
                refs.pop(0)
            out_ref, acc, low, mask = refs
        else:
            acc, low = refs
        n, k = pl.program_id(0), pl.program_id(1)
        at = 0
        for i, t in enumerate(xs):
            mine = x_refs[at : at + len(t)]
            at += len(t)

            @pl.when(k == i)
            def _():
                x = mine[0][...]
                for other in mine[1:]:
                    x = x + other[...]
                p = jnp.dot(x, w_ref[...], preferred_element_type=f32)
                if i == 0 and carry is not None:
                    p = p + acc_in[...]
                acc[...] = p if i == 0 else acc[...] + p

                @pl.when(n == 0)
                def _():
                    q = dot_t(x, down_ref[...])
                    if i == 0 and carry is not None:
                        q = q + low_in[...]
                    low[...] = q if i == 0 else low[...] + q

        if finish is not None:

            @pl.when(jnp.logical_and(n == 0, k == steps - 1))
            def _():
                total = low[...]
                if has_partial:
                    sent = part_ref[:, features : features + lanes].astype(f32)
                    total = total + jnp.concatenate([sent] * (pool_rows // lanes), axis=1)
                chosen = ids_ref[...] == owner_ref[...]
                mask[...] = jnp.where(chosen, total, 0.0).astype(bf16)

            @pl.when(k == steps - 1)
            def _():
                y = adapter_scale * jnp.dot(mask[...], up_ref[...], preferred_element_type=f32)
                y = y + acc[...]
                if has_partial:
                    y = y + part_ref[:, pl.ds(pl.multiple_of(n * tile, tile), tile)].astype(f32)
                out_ref[...] = y.astype(bf16)

    whole = lambda shape: pl.BlockSpec(shape, lambda n, k, row: (0, 0))
    in_specs = [whole((rows, step)) for _ in flat]
    operands = list(flat)
    in_specs += [
        pl.BlockSpec((step, tile), lambda n, k, row: (first + k, n)),
        pl.BlockSpec(
            (pool_rows, step),
            lambda n, k, row: (0, jnp.where(n == 0, first + k, first + steps - 1)),
        ),
    ]
    operands += [weight, pool]
    if carry is not None:
        in_specs += [
            pl.BlockSpec((rows, tile), lambda n, k, row: (0, n)),
            whole((rows, pool_rows)),
        ]
        operands += list(carry)
    aliases = {}
    if finish is None:
        row = jnp.zeros((1,), jnp.int32)
        out_shape = [
            jax.ShapeDtypeStruct((rows, features), f32),
            jax.ShapeDtypeStruct((rows, pool_rows), f32),
        ]
        out_specs = [
            pl.BlockSpec((rows, tile), lambda n, k, row: (0, n)),
            whole((rows, pool_rows)),
        ]
        scratch = []
    else:
        row = finish["row"].reshape(1)
        in_specs += [
            pl.BlockSpec((pool_rows, tile), lambda n, k, row: (0, width // tile + n)),
            whole((1, pool_rows)),
            pl.BlockSpec((rows, 1), lambda n, k, row: (row[0], 0)),
        ]
        operands += [pool, finish["owner"], finish["ids"]]
        if has_partial:
            in_specs.append(whole((rows, features + lanes)))
            operands.append(finish["partial"])
        if has_prev:
            in_specs.append(pl.BlockSpec(memory_space=pl.ANY))
            operands.append(finish["prev"])
            aliases = {len(operands): 0}
        out_shape = jax.ShapeDtypeStruct((finish["ids"].shape[0], features), bf16)
        out_specs = pl.BlockSpec((rows, tile), lambda n, k, row: (row[0], n))
        scratch = [
            pltpu.VMEM((rows, tile), f32),
            pltpu.VMEM((rows, pool_rows), f32),
            pltpu.VMEM((rows, pool_rows), bf16),
        ]
    flops = 2 * rows * steps * step * (features + pool_rows)
    return pl.pallas_call(
        kernel,
        grid_spec=pltpu.PrefetchScalarGridSpec(
            num_scalar_prefetch=1,
            grid=(tiles, steps),
            in_specs=in_specs,
            out_specs=out_specs,
            scratch_shapes=scratch,
        ),
        out_shape=out_shape,
        input_output_aliases=aliases,
        compiler_params=pltpu.CompilerParams(vmem_limit_bytes=vmem),
        cost_estimate=pl.CostEstimate(
            flops=flops, bytes_accessed=2 * steps * step * features, transcendentals=0
        ),
        name="product",
    )(row, *operands)


def partial_product(chunks, slabs, places, row, ids, owner, pool):
    rows, step = chunks[0].shape
    features = slabs[0][0].shape[1]
    pool_rows = pool.shape[0]
    tile = 512
    tiles = features // tile
    count = len(chunks)
    flat = [a for s in slabs for a in s]
    per = len(slabs[0])
    span = slabs[0][0].shape[0]

    def kernel(row_ref, place_ref, *refs):
        x_refs = refs[:count]
        w_refs = refs[count : count + len(flat)]
        down_ref, owner_ref, ids_ref, out_ref, moved = refs[count + len(flat) :]
        n = pl.program_id(0)

        @pl.when(n == 0)
        def _():
            low = None
            for s in range(count):
                for j in range(step // lanes):
                    off = pl.multiple_of(place_ref[j] * lanes, lanes)
                    moved[s, :, j * lanes : (j + 1) * lanes] = x_refs[s][:, pl.ds(off, lanes)]
                q = dot_t(x_refs[s][...], down_ref[:, s * step : (s + 1) * step])
                low = q if low is None else low + q
            low = jnp.where(ids_ref[...] == owner_ref[...], low, 0.0)
            sent = low[:, :lanes]
            for j in range(1, pool_rows // lanes):
                sent = sent + low[:, j * lanes : (j + 1) * lanes]
            out_ref[:, features:] = sent.astype(bf16)

        total = None
        for s in range(count):
            for i in range(per):
                x = moved[s, :, i * span : (i + 1) * span]
                p = jnp.dot(x, w_refs[s * per + i][...], preferred_element_type=f32)
                total = p if total is None else total + p
        out_ref[:, pl.ds(pl.multiple_of(n * tile, tile), tile)] = total.astype(bf16)

    whole = lambda shape: pl.BlockSpec(shape, lambda n, row, place: (0, 0))
    return pl.pallas_call(
        kernel,
        grid_spec=pltpu.PrefetchScalarGridSpec(
            num_scalar_prefetch=2,
            grid=(tiles,),
            in_specs=[whole((rows, step))] * count
            + [pl.BlockSpec((span, tile), lambda n, row, place: (0, n))] * len(flat)
            + [
                whole((pool_rows, count * step)),
                whole((1, pool_rows)),
                pl.BlockSpec((rows, 1), lambda n, row, place: (row[0], 0)),
            ],
            out_specs=whole((rows, features + lanes)),
            scratch_shapes=[pltpu.VMEM((count, rows, step), bf16)],
        ),
        out_shape=jax.ShapeDtypeStruct((rows, features + lanes), bf16),
        compiler_params=pltpu.CompilerParams(vmem_limit_bytes=vmem),
        cost_estimate=pl.CostEstimate(
            flops=2 * rows * count * step * features,
            bytes_accessed=2 * count * step * features,
            transcendentals=0,
        ),
        name="partial_product",
    )(row.reshape(1), places, *chunks, *flat, pool, owner, ids)


def body(
    layer_input,
    input_norm_weight,
    query_base_matrix,
    adapter_down_weight,
    adapter_up_weight,
    token_adapter_index,
):
    rank = adapter_down_weight.shape[2]
    parts = 4
    step = layer_input.shape[1] // parts
    t = lax.axis_index("tensor")
    r = lax.axis_index("replica")
    q = lax.axis_index("groups") * 4 + r
    inward = lambda a: lax.ppermute(a, "tensor", [(0, 1), (3, 2)])
    outward = lambda a: lax.ppermute(a, "tensor", [(1, 0), (2, 3)])
    cross = lambda a: lax.ppermute(a, "tensor", [(1, 2), (2, 1)])
    swap_y = lambda a: lax.ppermute(a, "groups", [(0, 1), (1, 0)])
    swap_x = lambda a: lax.ppermute(a, "replica", [(i, i ^ 2) for i in range(4)])
    swap_core = lambda a: lax.ppermute(a, "replica", [(i, i ^ 1) for i in range(4)])

    piece = step // 8
    half = piece // 2
    sent = [
        inward(lax.dynamic_slice_in_dim(query_base_matrix, s * step + q * piece, piece, 0))
        for s in range(2)
    ]

    pool = jnp.concatenate([adapter_down_weight[0].T, adapter_up_weight[0]], axis=1)
    pool = jnp.concatenate([pool, swap_x(pool)], axis=0)
    pool = jnp.concatenate([pool, swap_core(pool)], axis=0)
    owner = jnp.repeat(jnp.stack([r, r ^ 2, r ^ 1, r ^ 3]), rank).astype(jnp.int32)[None, :]
    ids = token_adapter_index[:, None]

    own = norm_chunks(layer_input, input_norm_weight[None, :], parts)
    order = (2, 3, 0, 1)
    out_own = {k: outward(own[k]) for k in (2, 3)}
    mid = {k: cross(own[k]) for k in order}
    end = {k: inward(own[k]) for k in order}
    out_mid = {k: outward(mid[k]) for k in (2, 3)}
    far = {k: cross(end[k]) for k in order}
    out_far = {k: outward(far[k]) for k in (2, 3)}

    slabs = []
    for s in range(2):
        a, b = sent[s][:half], sent[s][half:]
        a = jnp.concatenate([a, swap_y(a)], axis=0)
        b = jnp.concatenate([b, swap_x(b)], axis=0)
        mine = jnp.concatenate([a, swap_x(a), b, swap_y(b)], axis=0)
        slabs.append([mine, swap_core(mine)])
    places = []
    for o in (q, q ^ 1):
        places += [2 * o, 2 * (o ^ 4), 2 * (o ^ 2), 2 * (o ^ 6)]
        places += [2 * o + 1, 2 * (o ^ 2) + 1, 2 * (o ^ 4) + 1, 2 * (o ^ 6) + 1]
    places = jnp.stack(places).astype(jnp.int32)

    mid_row = jnp.where(t < 2, 2, 1).astype(jnp.int32)
    far_row = jnp.where(t < 2, 3, 0).astype(jnp.int32)
    t = t.astype(jnp.int32)

    def help_with(x, row):
        return outward(partial_product([x[0], x[1]], slabs, places, row, ids, owner, pool))

    def finish(row, partial, prev):
        return dict(row=row, partial=partial, prev=prev, owner=owner, ids=ids)

    part_own = help_with(own, t)
    part_mid = help_with(mid, mid_row)
    part_far = help_with(far, far_row)

    w = query_base_matrix
    out = product(0, [(own[k],) for k in range(4)], w, pool, None, finish(t, None, None))
    xs = [(end[0],), (end[1],), (end[2], out_own[2]), (end[3], out_own[3])]
    out = product(0, xs, w, pool, None, finish(t ^ 1, part_own, out))
    xs = [(mid[0],), (mid[1],), (mid[2], out_mid[2]), (mid[3], out_mid[3])]
    out = product(0, xs, w, pool, None, finish(mid_row, part_mid, out))
    carry = product(0, [(far[0],), (far[1],)], w, pool)
    xs = [(far[2], out_far[2]), (far[3], out_far[3])]
    return product(2, xs, w, pool, carry, finish(far_row, part_far, out))


def solution(mesh):
    placed = (
        P(("groups", "replica", "tensor"), None),
        P(),
        P(None, "tensor"),
        P("replica", None, None),
        P("replica", None, "tensor"),
        P(("groups", "replica")),
    )
    line = mesh.shape["tensor"] == 4 and mesh.shape["replica"] == 4 and mesh.shape["groups"] == 2
    return jax.shard_map(
        body if line else plain,
        mesh=mesh,
        in_specs=placed,
        out_specs=P(("groups", "replica"), "tensor"),
        check_vma=False,
    )
```

```python
import jax
import jax.numpy as jnp
from jax import lax
from jax.experimental import pallas as pl
from jax.experimental.pallas import tpu as pltpu
from jax.sharding import PartitionSpec as P

adapter_scale = 2.0
lanes = 128
vmem = 48 * 1024 * 1024
f32 = jnp.float32
bf16 = jnp.bfloat16


def plain(
    layer_input,
    input_norm_weight,
    query_base_matrix,
    adapter_down_weight,
    adapter_up_weight,
    token_adapter_index,
):
    xf = layer_input.astype(f32)
    ms = jnp.mean(xf * xf, axis=-1, keepdims=True)
    normed = (xf * lax.rsqrt(ms + 1e-05) * input_norm_weight.astype(f32)).astype(bf16)
    gathered = lax.all_gather(normed, "tensor", axis=0, tiled=True)
    down_all = lax.all_gather(adapter_down_weight, "replica", axis=0, tiled=True)
    up_all = lax.all_gather(adapter_up_weight, "replica", axis=0, tiled=True)
    count, width, rank = down_all.shape
    down_cat = jnp.transpose(down_all, (1, 0, 2)).reshape(width, count * rank)
    low_all = jnp.dot(gathered, down_cat, preferred_element_type=f32)
    owner = jnp.repeat(jnp.arange(count, dtype=jnp.int32), rank)
    chosen = token_adapter_index[:, None] == owner[None, :]
    masked = jnp.where(chosen, low_all, 0.0).astype(bf16)
    update = jnp.dot(
        masked, up_all.reshape(count * rank, up_all.shape[2]), preferred_element_type=f32
    )
    base = jnp.dot(gathered, query_base_matrix, preferred_element_type=f32)
    return (base + adapter_scale * update).astype(bf16)


def norm_chunks(x, gain, spans):
    rows, width = x.shape
    block = 48

    def kernel(x_ref, g_ref, *out_refs):
        xf = x_ref[...].astype(f32)
        ms = jnp.mean(xf * xf, axis=-1, keepdims=True)
        y = (xf * lax.rsqrt(ms + 1e-05) * g_ref[...].astype(f32)).astype(bf16)
        for (lo, hi), out_ref in zip(spans, out_refs):
            out_ref[...] = y[:, lo:hi]

    return pl.pallas_call(
        kernel,
        grid=(rows // block,),
        in_specs=[
            pl.BlockSpec((block, width), lambda i: (i, 0)),
            pl.BlockSpec((1, width), lambda i: (0, 0)),
        ],
        out_specs=[pl.BlockSpec((block, hi - lo), lambda i: (i, 0)) for lo, hi in spans],
        out_shape=[jax.ShapeDtypeStruct((rows, hi - lo), bf16) for lo, hi in spans],
        compiler_params=pltpu.CompilerParams(vmem_limit_bytes=vmem),
        cost_estimate=pl.CostEstimate(flops=1000, bytes_accessed=1000, transcendentals=0),
        name="norm_chunks",
    )(x, gain)


def dot_t(a, b):
    return lax.dot_general(a, b, (((1,), (1,)), ((), ())), preferred_element_type=f32)


def after(x, *others):
    return lax.optimization_barrier((x, *others))[0]


def constant(shape):
    return pl.BlockSpec(shape, lambda *_: (0, 0), pipeline_mode=pl.Buffered(1))


def product(pieces, rows, depth, weight, pool=None, choose=None):
    features = weight.shape[1]
    pool_rows = 0 if pool is None else pool.shape[0]
    tile = 256
    tiles = features // tile
    whole = lambda a: a if isinstance(a, tuple) else (a, 0, a.shape[1])
    pieces = [(r, f, [whole(a) for a in arrays]) for r, f, arrays in pieces]
    flat = []
    for _, _, arrays in pieces:
        flat += [a for a, _, _ in arrays if not any(a is b for b in flat)]

    def kernel(*refs):
        refs = list(refs)
        x_refs = [refs.pop(0) for _ in flat]
        w_ref = refs.pop(0)
        if pool is not None:
            down_ref = refs.pop(0)
        if choose is not None:
            owner_ref, ids_ref = refs.pop(0), refs.pop(0)
        if pool is not None:
            sem, held = refs.pop(), refs.pop()
            fetch = pltpu.make_async_copy(down_ref.at[:, pl.ds(0, depth)], held, sem)
        xs = refs.pop()
        out_ref = refs.pop(0)
        n = pl.program_id(0)

        @pl.when(n == 0)
        def _():
            for row, feature, arrays in pieces:
                x = None
                for a, lo, hi in arrays:
                    (at,) = [i for i, b in enumerate(flat) if a is b]
                    y = x_refs[at][:, lo:hi]
                    x = y if x is None else x + y
                xs[row : row + x.shape[0], feature : feature + x.shape[1]] = x
            if pool is not None:
                fetch.start()

        p = jnp.dot(xs[...], w_ref[...], preferred_element_type=f32)
        if choose is None:
            out_ref[...] = p
        else:
            out_ref[:, pl.ds(pl.multiple_of(n * tile, tile), tile)] = p.astype(bf16)

        if pool is not None:

            @pl.when(n == tiles - 1)
            def _():
                fetch.wait()
                low = dot_t(xs[...], held[...])
                if choose is None:
                    refs[0][...] = low
                else:
                    low = jnp.where(ids_ref[...] == owner_ref[...], low, 0.0)
                    chosen = low[:, :lanes]
                    for j in range(1, pool_rows // lanes):
                        chosen = chosen + low[:, j * lanes : (j + 1) * lanes]
                    out_ref[:, features:] = chosen.astype(bf16)

    in_specs = [constant(a.shape) for a in flat]
    in_specs += [pl.BlockSpec((depth, tile), lambda n: (0, n))]
    operands = flat + [weight]
    if pool is not None:
        in_specs.append(pl.BlockSpec(memory_space=pl.ANY))
        operands.append(pool)
    if pool is None:
        out_shape = jax.ShapeDtypeStruct((rows, features), f32)
        out_specs = pl.BlockSpec((rows, tile), lambda n: (0, n))
    elif choose is None:
        out_shape = [
            jax.ShapeDtypeStruct((rows, features), f32),
            jax.ShapeDtypeStruct((rows, pool_rows), f32),
        ]
        out_specs = [
            pl.BlockSpec((rows, tile), lambda n: (0, n)),
            pl.BlockSpec((rows, pool_rows), lambda n: (0, 0)),
        ]
    else:
        owner, ids = choose
        in_specs += [constant((1, pool_rows)), constant((rows, 1))]
        operands += [owner, ids]
        out_shape = jax.ShapeDtypeStruct((rows, features + lanes), bf16)
        out_specs = pl.BlockSpec((rows, features + lanes), lambda n: (0, 0))
    scratch = [pltpu.VMEM((rows, depth), bf16)]
    if pool is not None:
        scratch += [pltpu.VMEM((pool_rows, depth), bf16), pltpu.SemaphoreType.DMA(())]
    return pl.pallas_call(
        kernel,
        grid=(tiles,),
        in_specs=in_specs,
        out_specs=out_specs,
        out_shape=out_shape,
        scratch_shapes=scratch,
        compiler_params=pltpu.CompilerParams(vmem_limit_bytes=vmem),
        cost_estimate=pl.CostEstimate(flops=1000, bytes_accessed=1000, transcendentals=0),
        name="product" if choose is None else "product_sent",
    )(*operands)


def finish(acc, low, at, partial, part_at, pool, width, owner, ids, row, rows, prev):
    features = acc.shape[1]
    pool_rows = pool.shape[0]
    tile = 512
    tiles = features // tile

    def kernel(row_ref, *refs):
        refs = list(refs)
        acc_ref, low_ref, up_ref, owner_ref, ids_ref = [refs.pop(0) for _ in range(5)]
        if partial is not None:
            part_ref, sent_ref = refs.pop(0), refs.pop(0)
        if prev is not None:
            refs.pop(0)
        (out_ref,) = refs
        total = low_ref[...]
        y = acc_ref[...]
        if partial is not None:
            sent = sent_ref[...].astype(f32)
            total = total + jnp.concatenate([sent] * (pool_rows // lanes), axis=1)
            y = y + part_ref[...].astype(f32)
        mask = jnp.where(ids_ref[...] == owner_ref[...], total, 0.0).astype(bf16)
        y = y + adapter_scale * jnp.dot(mask, up_ref[...], preferred_element_type=f32)
        out_ref[...] = y.astype(bf16)

    in_specs = [
        pl.BlockSpec((rows, tile), lambda n, r: (at, n)),
        pl.BlockSpec((rows, pool_rows), lambda n, r: (at, 0)),
        pl.BlockSpec((pool_rows, tile), lambda n, r: (0, width // tile + n)),
        pl.BlockSpec((1, pool_rows), lambda n, r: (0, 0)),
        pl.BlockSpec((rows, 1), lambda n, r: (r[0], 0)),
    ]
    operands = [acc, low, pool, owner, ids]
    if partial is not None:
        in_specs += [
            pl.BlockSpec((rows, tile), lambda n, r: (part_at, n)),
            pl.BlockSpec((rows, lanes), lambda n, r: (part_at, features // lanes)),
        ]
        operands += [partial, partial]
    aliases = {}
    if prev is not None:
        in_specs.append(pl.BlockSpec(memory_space=pl.ANY))
        operands.append(prev)
        aliases = {len(operands): 0}
    return pl.pallas_call(
        kernel,
        grid_spec=pltpu.PrefetchScalarGridSpec(
            num_scalar_prefetch=1,
            grid=(tiles,),
            in_specs=in_specs,
            out_specs=pl.BlockSpec((rows, tile), lambda n, r: (r[0], n)),
        ),
        out_shape=jax.ShapeDtypeStruct((ids.shape[0], features), bf16),
        input_output_aliases=aliases,
        compiler_params=pltpu.CompilerParams(vmem_limit_bytes=vmem),
        cost_estimate=pl.CostEstimate(flops=1000, bytes_accessed=1000, transcendentals=0),
        name="finish",
    )(row.reshape(1), *operands)


def body(
    layer_input,
    input_norm_weight,
    query_base_matrix,
    adapter_down_weight,
    adapter_up_weight,
    token_adapter_index,
):
    rows, width = layer_input.shape
    count = lax.axis_size("replica")
    rank = adapter_down_weight.shape[2]
    t = lax.axis_index("tensor").astype(jnp.int32)
    q = lax.axis_index("groups") * count + lax.axis_index("replica")
    inward = lambda a: lax.ppermute(a, "tensor", [(0, 1), (3, 2)])
    outward = lambda a: lax.ppermute(a, "tensor", [(1, 0), (2, 3)])
    cross = lambda a: lax.ppermute(a, "tensor", [(1, 2), (2, 1)])

    h = width * 7 // 16
    m = (width + h) // 2
    piece = h // (count * lax.axis_size("groups"))
    share = lax.dynamic_slice_in_dim(query_base_matrix, q * piece, piece, 0)
    sent = inward(share)
    layer_input = after(layer_input, share)
    adapter_down_weight = after(adapter_down_weight, share)

    pool = jnp.concatenate([adapter_down_weight[0].T, adapter_up_weight[0]], axis=1)
    pool = lax.all_gather(pool, "replica", axis=0, tiled=True)
    owner = jnp.repeat(jnp.arange(count, dtype=jnp.int32), rank)[None, :]
    ids = token_adapter_index[:, None]

    own_h, own_d, own_d0, own_d1 = norm_chunks(
        layer_input, input_norm_weight[None, :], [(0, h), (h, width), (h, m), (m, width)]
    )
    w = query_base_matrix
    own = product([(0, 0, [own_h]), (0, h, [own_d])], rows, width, w)
    out_own = outward(own_d)
    mid_d = cross(own_d)
    end_d0 = inward(after(own_d0, sent))
    out_mid = outward(after(mid_d, out_own))
    mid_h = cross(after(own_h, mid_d, own))
    mid_row = jnp.where(t < 2, 2, 1).astype(jnp.int32)
    far_row = jnp.where(t < 2, 3, 0).astype(jnp.int32)
    last = (pool, width, owner, ids)
    own_low = dot_t(own_h, pool[:, :h]) + dot_t(own_d, pool[:, h:width])
    out = finish(own, own_low, 0, None, 0, *last, t, rows, None)
    end_d1 = inward(after(own_d1, end_d0, out))
    far_d0 = cross(after(end_d0, mid_h))
    end_h = inward(after(own_h, end_d1))
    out_far0 = outward(after(far_d0, out_mid))
    far_d1 = cross(after(end_d1, far_d0))
    mid = product(
        [(0, 0, [mid_h]), (0, h, [after(mid_d, far_d0), out_mid])], rows, width, w, pool
    )
    out_far1 = outward(after(far_d1, out_far0, mid[0]))
    far_h = cross(after(end_h, far_d1))
    sent = after(sent, mid_d, out_own, own)
    help_weight = lax.all_gather(sent, ("groups", "replica"), axis=0, tiled=True)

    pick = lambda row: lax.dynamic_slice_in_dim(ids, row * rows, rows, 0)
    ids_near = jnp.concatenate([pick(t), pick(mid_row)], axis=0)
    part_near = product(
        [(0, 0, [own_h]), (rows, 0, [mid_h])], 2 * rows, h, help_weight, pool,
        (owner, ids_near),
    )
    far_h = after(far_h, part_near)
    part_near = outward(after(part_near, out_far1))
    part_far = product([(0, 0, [far_h])], rows, h, help_weight, pool, (owner, pick(far_row)))
    far_h = after(far_h, part_far)
    part_far = outward(part_far)
    cut = m - h
    distant = product(
        [
            (0, 0, [end_h]),
            (0, h, [end_d0, (out_own, 0, cut)]),
            (0, m, [end_d1, (out_own, cut, width - h)]),
            (rows, 0, [far_h]),
            (rows, h, [far_d0, out_far0]),
            (rows, m, [far_d1, out_far1]),
        ],
        2 * rows, width, w, pool,
    )
    out = finish(*mid, 0, part_near, 1, *last, mid_row, rows, out)
    out = finish(*distant, 0, part_near, 0, *last, t ^ 1, rows, out)
    return finish(*distant, 1, part_far, 0, *last, far_row, rows, out)


def solution(mesh):
    placed = (
        P(("groups", "replica", "tensor"), None),
        P(),
        P(None, "tensor"),
        P("replica", None, None),
        P("replica", None, "tensor"),
        P(("groups", "replica")),
    )
    line = mesh.shape["tensor"] == 4 and mesh.shape["replica"] == 4 and mesh.shape["groups"] == 2
    return jax.shard_map(
        body if line else plain,
        mesh=mesh,
        in_specs=placed,
        out_specs=P(("groups", "replica"), "tensor"),
        check_vma=False,
    )
```

```python
import jax
import jax.numpy as jnp
from jax import lax
from jax.experimental import pallas as pl
from jax.experimental.pallas import tpu as pltpu
from jax.sharding import PartitionSpec as P

adapter_scale = 2.0
lanes = 128
vmem = 48 * 1024 * 1024
f32 = jnp.float32
bf16 = jnp.bfloat16


def plain(
    layer_input,
    input_norm_weight,
    query_base_matrix,
    adapter_down_weight,
    adapter_up_weight,
    token_adapter_index,
):
    xf = layer_input.astype(f32)
    ms = jnp.mean(xf * xf, axis=-1, keepdims=True)
    normed = (xf * lax.rsqrt(ms + 1e-05) * input_norm_weight.astype(f32)).astype(bf16)
    gathered = lax.all_gather(normed, "tensor", axis=0, tiled=True)
    down_all = lax.all_gather(adapter_down_weight, "replica", axis=0, tiled=True)
    up_all = lax.all_gather(adapter_up_weight, "replica", axis=0, tiled=True)
    count, width, rank = down_all.shape
    down_cat = jnp.transpose(down_all, (1, 0, 2)).reshape(width, count * rank)
    low_all = jnp.dot(gathered, down_cat, preferred_element_type=f32)
    owner = jnp.repeat(jnp.arange(count, dtype=jnp.int32), rank)
    chosen = token_adapter_index[:, None] == owner[None, :]
    masked = jnp.where(chosen, low_all, 0.0).astype(bf16)
    update = jnp.dot(
        masked, up_all.reshape(count * rank, up_all.shape[2]), preferred_element_type=f32
    )
    base = jnp.dot(gathered, query_base_matrix, preferred_element_type=f32)
    return (base + adapter_scale * update).astype(bf16)


def norm_chunks(x, gain, spans):
    rows, width = x.shape
    block = 48

    def kernel(x_ref, g_ref, *out_refs):
        xf = x_ref[...].astype(f32)
        ms = jnp.mean(xf * xf, axis=-1, keepdims=True)
        y = (xf * lax.rsqrt(ms + 1e-05) * g_ref[...].astype(f32)).astype(bf16)
        for (lo, hi), out_ref in zip(spans, out_refs):
            out_ref[...] = y[:, lo:hi]

    return pl.pallas_call(
        kernel,
        grid=(rows // block,),
        in_specs=[
            pl.BlockSpec((block, width), lambda i: (i, 0)),
            pl.BlockSpec((1, width), lambda i: (0, 0)),
        ],
        out_specs=[pl.BlockSpec((block, hi - lo), lambda i: (i, 0)) for lo, hi in spans],
        out_shape=[jax.ShapeDtypeStruct((rows, hi - lo), bf16) for lo, hi in spans],
        compiler_params=pltpu.CompilerParams(vmem_limit_bytes=vmem),
        cost_estimate=pl.CostEstimate(flops=1000, bytes_accessed=1000, transcendentals=0),
        name="norm_chunks",
    )(x, gain)


def dot_t(a, b):
    return lax.dot_general(a, b, (((1,), (1,)), ((), ())), preferred_element_type=f32)


def after(x, *others):
    return lax.optimization_barrier((x, *others))[0]


def constant(shape):
    return pl.BlockSpec(shape, lambda *_: (0, 0), pipeline_mode=pl.Buffered(1))


def product(pieces, rows, first, weights, pool=None, choose=None, carry=None, flops=1000):
    features = weights[0][0].shape[1]
    depth = sum(count for _, _, count in weights)
    pool_rows = 0 if pool is None else pool.shape[0]
    tile = 256
    tiles = features // tile
    whole = lambda a: a if isinstance(a, tuple) else (a, 0, a.shape[1])
    pieces = [(r, f, [whole(a) for a in arrays]) for r, f, arrays in pieces]
    flat = []
    for _, _, arrays in pieces:
        flat += [a for a, _, _ in arrays if not any(a is b for b in flat)]

    def kernel(*refs):
        refs = list(refs)
        take = lambda count: [refs.pop(0) for _ in range(count)]
        x_refs, w_refs = take(len(flat)), take(len(weights))
        if pool is not None:
            (down_ref,) = take(1)
        if choose is not None:
            owner_ref, ids_ref = take(2)
        if carry is not None:
            acc_ref, sum_ref = take(2)
        (out_ref,) = take(1)
        if pool is not None and choose is None:
            (low_ref,) = take(1)
        (xs,) = take(1)
        if pool is not None:
            held, sem = take(2)
            fetch = pltpu.make_async_copy(down_ref.at[:, pl.ds(first, depth)], held, sem)
        n = pl.program_id(0)

        @pl.when(n == 0)
        def _():
            for row, feature, arrays in pieces:
                x = None
                for a, lo, hi in arrays:
                    (at,) = [i for i, b in enumerate(flat) if a is b]
                    y = x_refs[at][:, lo:hi]
                    x = y if x is None else x + y
                at = feature - first
                xs[row : row + x.shape[0], at : at + x.shape[1]] = x
            if pool is not None:
                fetch.start()

        p = None
        at = 0
        for w_ref in w_refs:
            x = xs[:, at : at + w_ref.shape[0]]
            at += w_ref.shape[0]
            y = jnp.dot(x, w_ref[...], preferred_element_type=f32)
            p = y if p is None else p + y
        if choose is not None:
            out_ref[:, pl.ds(pl.multiple_of(n * tile, tile), tile)] = p.astype(bf16)
        elif carry is not None:
            out_ref[...] = p + acc_ref[...]
        else:
            out_ref[...] = p

        if pool is not None:

            @pl.when(n == tiles - 1)
            def _():
                fetch.wait()
                low = dot_t(xs[...], held[...])
                if carry is not None:
                    low = low + sum_ref[...]
                if choose is None:
                    low_ref[...] = low
                else:
                    low = jnp.where(ids_ref[...] == owner_ref[...], low, 0.0)
                    chosen = low[:, :lanes]
                    for j in range(1, pool_rows // lanes):
                        chosen = chosen + low[:, j * lanes : (j + 1) * lanes]
                    out_ref[:, features:] = chosen.astype(bf16)

    in_specs = [constant(a.shape) for a in flat]
    operands = list(flat)
    for array, row, count in weights:
        if row % count == 0:
            spec = pl.BlockSpec((count, tile), lambda n, at=row // count: (at, n))
        else:
            spec = pl.BlockSpec(
                (pl.Element(count), pl.Element(tile)), lambda n, at=row: (at, n * tile)
            )
        in_specs.append(spec)
        operands.append(array)
    if pool is not None:
        in_specs.append(pl.BlockSpec(memory_space=pl.ANY))
        operands.append(pool)
    if choose is not None:
        owner, ids = choose
        in_specs += [constant((1, pool_rows)), constant((rows, 1))]
        operands += [owner, ids]
    if carry is not None:
        in_specs += [pl.BlockSpec((rows, tile), lambda n: (0, n)), constant((rows, pool_rows))]
        operands += list(carry)
    if choose is not None:
        out_shape = jax.ShapeDtypeStruct((rows, features + lanes), bf16)
        out_specs = pl.BlockSpec((rows, features + lanes), lambda n: (0, 0))
    else:
        out_shape = jax.ShapeDtypeStruct((rows, features), f32)
        out_specs = pl.BlockSpec((rows, tile), lambda n: (0, n))
        if pool is not None:
            out_shape = [out_shape, jax.ShapeDtypeStruct((rows, pool_rows), f32)]
            out_specs = [out_specs, pl.BlockSpec((rows, pool_rows), lambda n: (0, 0))]
    scratch = [pltpu.VMEM((rows, depth), bf16)]
    if pool is not None:
        scratch += [pltpu.VMEM((pool_rows, depth), bf16), pltpu.SemaphoreType.DMA(())]
    return pl.pallas_call(
        kernel,
        grid=(tiles,),
        in_specs=in_specs,
        out_specs=out_specs,
        out_shape=out_shape,
        scratch_shapes=scratch,
        compiler_params=pltpu.CompilerParams(vmem_limit_bytes=vmem),
        cost_estimate=pl.CostEstimate(flops=flops, bytes_accessed=1000, transcendentals=0),
        name="product" if choose is None else "product_sent",
    )(*operands)


def finish(acc, low, at, partial, part_at, pool, width, owner, ids, row, rows, prev):
    features = acc.shape[1]
    pool_rows = pool.shape[0]
    tile = 512
    tiles = features // tile

    def kernel(row_ref, *refs):
        refs = list(refs)
        acc_ref, low_ref, up_ref, owner_ref, ids_ref = [refs.pop(0) for _ in range(5)]
        if partial is not None:
            part_ref, sent_ref = refs.pop(0), refs.pop(0)
        if prev is not None:
            refs.pop(0)
        (out_ref,) = refs
        total = low_ref[...]
        y = acc_ref[...]
        if partial is not None:
            sent = sent_ref[...].astype(f32)
            total = total + jnp.concatenate([sent] * (pool_rows // lanes), axis=1)
            y = y + part_ref[...].astype(f32)
        mask = jnp.where(ids_ref[...] == owner_ref[...], total, 0.0).astype(bf16)
        y = y + adapter_scale * jnp.dot(mask, up_ref[...], preferred_element_type=f32)
        out_ref[...] = y.astype(bf16)

    in_specs = [
        pl.BlockSpec((rows, tile), lambda n, r: (at, n)),
        pl.BlockSpec((rows, pool_rows), lambda n, r: (at, 0)),
        pl.BlockSpec((pool_rows, tile), lambda n, r: (0, width // tile + n)),
        pl.BlockSpec((1, pool_rows), lambda n, r: (0, 0)),
        pl.BlockSpec((rows, 1), lambda n, r: (r[0], 0)),
    ]
    operands = [acc, low, pool, owner, ids]
    if partial is not None:
        in_specs += [
            pl.BlockSpec((rows, tile), lambda n, r: (part_at, n)),
            pl.BlockSpec((rows, lanes), lambda n, r: (part_at, features // lanes)),
        ]
        operands += [partial, partial]
    aliases = {}
    if prev is not None:
        in_specs.append(pl.BlockSpec(memory_space=pl.ANY))
        operands.append(prev)
        aliases = {len(operands): 0}
    return pl.pallas_call(
        kernel,
        grid_spec=pltpu.PrefetchScalarGridSpec(
            num_scalar_prefetch=1,
            grid=(tiles,),
            in_specs=in_specs,
            out_specs=pl.BlockSpec((rows, tile), lambda n, r: (r[0], n)),
        ),
        out_shape=jax.ShapeDtypeStruct((ids.shape[0], features), bf16),
        input_output_aliases=aliases,
        compiler_params=pltpu.CompilerParams(vmem_limit_bytes=vmem),
        cost_estimate=pl.CostEstimate(flops=1000, bytes_accessed=1000, transcendentals=0),
        name="finish",
    )(row.reshape(1), *operands)


def body(
    layer_input,
    input_norm_weight,
    query_base_matrix,
    adapter_down_weight,
    adapter_up_weight,
    token_adapter_index,
):
    rows, width = layer_input.shape
    count = lax.axis_size("replica")
    rank = adapter_down_weight.shape[2]
    t = lax.axis_index("tensor").astype(jnp.int32)
    q = lax.axis_index("groups") * count + lax.axis_index("replica")
    inward = lambda a: lax.ppermute(a, "tensor", [(0, 1), (3, 2)])
    outward = lambda a: lax.ppermute(a, "tensor", [(1, 0), (2, 3)])
    cross = lambda a: lax.ppermute(a, "tensor", [(1, 2), (2, 1)])


    h = width * 7 // 16
    m = (width + h) // 2
    piece = h // (count * lax.axis_size("groups"))
    share = lax.dynamic_slice_in_dim(query_base_matrix, q * piece, piece, 0)
    sent = inward(share)
    layer_input = after(layer_input, share)
    adapter_down_weight = after(adapter_down_weight, share)
    pool = jnp.concatenate([adapter_down_weight[0].T, adapter_up_weight[0]], axis=1)
    pool = lax.all_gather(pool, "replica", axis=0, tiled=True)
    owner = jnp.repeat(jnp.arange(count, dtype=jnp.int32), rank)[None, :]
    ids = token_adapter_index[:, None]

    own_h, own_d, own_d0, own_d1 = norm_chunks(
        layer_input, input_norm_weight[None, :], [(0, h), (h, width), (h, m), (m, width)]
    )
    w = [(query_base_matrix, 0, width)]
    own = product([(0, 0, [own_h]), (0, h, [own_d])], rows, 0, w)
    out_own = outward(own_d)
    mid_d = cross(own_d)
    end_d0 = inward(after(own_d0, sent))
    out_mid = outward(after(mid_d, out_own))
    mid_h = cross(after(own_h, mid_d, own))
    mid_row = jnp.where(t < 2, 2, 1).astype(jnp.int32)
    far_row = jnp.where(t < 2, 3, 0).astype(jnp.int32)
    last = (pool, width, owner, ids)
    own_low = dot_t(own_h, pool[:, :h]) + dot_t(own_d, pool[:, h:width])
    out = finish(own, own_low, 0, None, 0, *last, t, rows, None)
    end_d1 = inward(after(own_d1, end_d0, out))
    far_d0 = cross(after(end_d0, mid_h))
    end_h = inward(after(own_h, end_d1))
    out_far0 = outward(after(far_d0, out_mid))
    far_d1 = cross(after(end_d1, far_d0))
    mid = product(
        [(0, 0, [mid_h]), (0, h, [after(mid_d, far_d0), out_mid])], rows, 0, w, pool,
        flops=1000,
    )
    out_far1 = outward(after(far_d1, out_far0, mid[0]))
    far_h = cross(after(end_h, far_d1))
    sent = after(sent, mid_d, out_own, own)
    sent = lax.all_gather(sent, ("groups", "replica"), axis=0, tiled=True)
    help_weight = [(sent, 0, h)]

    pick = lambda row: lax.dynamic_slice_in_dim(ids, row * rows, rows, 0)
    ids_near = jnp.concatenate([pick(t), pick(mid_row)], axis=0)
    part_near = product(
        [(0, 0, [own_h]), (rows, 0, [mid_h])], 2 * rows, 0, help_weight, pool,
        (owner, ids_near),
    )
    distant = product(
        [
            (0, h, [after(end_d0, part_near), (out_own, 0, m - h)]),
            (0, m, [end_d1, (out_own, m - h, width - h)]),
            (rows, h, [far_d0, out_far0]),
            (rows, m, [far_d1, out_far1]),
        ],
        2 * rows, h, [(query_base_matrix, h, width - h)], pool,
    )
    part_near = outward(after(part_near, out_far1))
    far_h = after(far_h, distant[0])
    part_far = product([(0, 0, [far_h])], rows, 0, help_weight, pool, (owner, pick(far_row)))
    far_h = after(far_h, part_far)
    part_far = outward(part_far)
    distant = product(
        [(0, 0, [end_h]), (rows, 0, [far_h])],
        2 * rows, 0, [(query_base_matrix, 0, h)], pool, None, distant,
    )
    out = finish(*mid, 0, part_near, 1, *last, mid_row, rows, out)
    out = finish(*distant, 0, part_near, 0, *last, t ^ 1, rows, out)
    return finish(*distant, 1, part_far, 0, *last, far_row, rows, out)


def solution(mesh):
    placed = (
        P(("groups", "replica", "tensor"), None),
        P(),
        P(None, "tensor"),
        P("replica", None, None),
        P("replica", None, "tensor"),
        P(("groups", "replica")),
    )
    line = mesh.shape["tensor"] == 4 and mesh.shape["replica"] == 4 and mesh.shape["groups"] == 2
    return jax.shard_map(
        body if line else plain,
        mesh=mesh,
        in_specs=placed,
        out_specs=P(("groups", "replica"), "tensor"),
        check_vma=False,
    )
```

```python
import jax
import jax.numpy as jnp
from jax import lax
from jax.experimental import pallas as pl
from jax.experimental.pallas import tpu as pltpu
from jax.sharding import PartitionSpec as P

adapter_scale = 2.0
lanes = 128
vmem = 60 * 1024 * 1024
f32 = jnp.float32
bf16 = jnp.bfloat16


def plain(
    layer_input,
    input_norm_weight,
    query_base_matrix,
    adapter_down_weight,
    adapter_up_weight,
    token_adapter_index,
):
    xf = layer_input.astype(f32)
    ms = jnp.mean(xf * xf, axis=-1, keepdims=True)
    normed = (xf * lax.rsqrt(ms + 1e-05) * input_norm_weight.astype(f32)).astype(bf16)
    gathered = lax.all_gather(normed, "tensor", axis=0, tiled=True)
    down_all = lax.all_gather(adapter_down_weight, "replica", axis=0, tiled=True)
    up_all = lax.all_gather(adapter_up_weight, "replica", axis=0, tiled=True)
    count, width, rank = down_all.shape
    down_cat = jnp.transpose(down_all, (1, 0, 2)).reshape(width, count * rank)
    low_all = jnp.dot(gathered, down_cat, preferred_element_type=f32)
    owner = jnp.repeat(jnp.arange(count, dtype=jnp.int32), rank)
    chosen = token_adapter_index[:, None] == owner[None, :]
    masked = jnp.where(chosen, low_all, 0.0).astype(bf16)
    update = jnp.dot(
        masked, up_all.reshape(count * rank, up_all.shape[2]), preferred_element_type=f32
    )
    base = jnp.dot(gathered, query_base_matrix, preferred_element_type=f32)
    return (base + adapter_scale * update).astype(bf16)


def norm_chunks(x, gain, spans):
    rows, width = x.shape
    block = 48

    def kernel(x_ref, g_ref, *out_refs):
        xf = x_ref[...].astype(f32)
        ms = jnp.mean(xf * xf, axis=-1, keepdims=True)
        y = (xf * lax.rsqrt(ms + 1e-05) * g_ref[...].astype(f32)).astype(bf16)
        for (lo, hi), out_ref in zip(spans, out_refs):
            out_ref[...] = y[:, lo:hi]

    return pl.pallas_call(
        kernel,
        grid=(rows // block,),
        in_specs=[
            pl.BlockSpec((block, width), lambda i: (i, 0)),
            pl.BlockSpec((1, width), lambda i: (0, 0)),
        ],
        out_specs=[pl.BlockSpec((block, hi - lo), lambda i: (i, 0)) for lo, hi in spans],
        out_shape=[jax.ShapeDtypeStruct((rows, hi - lo), bf16) for lo, hi in spans],
        compiler_params=pltpu.CompilerParams(vmem_limit_bytes=vmem // 2),
        cost_estimate=pl.CostEstimate(flops=1000, bytes_accessed=1000, transcendentals=0),
        name="norm_chunks",
    )(x, gain)


def dot_t(a, b):
    return lax.dot_general(a, b, (((1,), (1,)), ((), ())), preferred_element_type=f32)


def after(x, *others):
    return lax.optimization_barrier((x, *others))[0]


def constant(shape):
    return pl.BlockSpec(shape, lambda *_: (0, 0), pipeline_mode=pl.Buffered(1))


def product(pieces, rows, first, weights, pool=None, choose=None, carry=None, flops=1000):
    features = weights[0][0].shape[1]
    depth = sum(count for _, _, count in weights)
    pool_rows = 0 if pool is None else pool.shape[0]
    tile = 256
    tiles = features // tile
    whole = lambda a: a if isinstance(a, tuple) else (a, 0, a.shape[1])
    pieces = [(r, f, [whole(a) for a in arrays]) for r, f, arrays in pieces]
    flat = []
    for _, _, arrays in pieces:
        flat += [a for a, _, _ in arrays if not any(a is b for b in flat)]

    def kernel(*refs):
        refs = list(refs)
        take = lambda count: [refs.pop(0) for _ in range(count)]
        x_refs, w_refs = take(len(flat)), take(len(weights))
        if pool is not None:
            (down_ref,) = take(1)
        if choose is not None:
            owner_ref, ids_ref = take(2)
        if carry is not None:
            acc_ref, sum_ref = take(2)
        (out_ref,) = take(1)
        if pool is not None and choose is None:
            (low_ref,) = take(1)
        (xs,) = take(1)
        if pool is not None:
            held, sem = take(2)
            fetch = pltpu.make_async_copy(down_ref.at[:, pl.ds(first, depth)], held, sem)
        n = pl.program_id(0)

        @pl.when(n == 0)
        def _():
            for row, feature, arrays in pieces:
                x = None
                for a, lo, hi in arrays:
                    (at,) = [i for i, b in enumerate(flat) if a is b]
                    y = x_refs[at][:, lo:hi]
                    x = y if x is None else x + y
                at = feature - first
                xs[row : row + x.shape[0], at : at + x.shape[1]] = x
            if pool is not None:
                fetch.start()

        p = None
        at = 0
        for w_ref in w_refs:
            x = xs[:, at : at + w_ref.shape[0]]
            at += w_ref.shape[0]
            y = jnp.dot(x, w_ref[...], preferred_element_type=f32)
            p = y if p is None else p + y
        if choose is not None:
            out_ref[:, pl.ds(pl.multiple_of(n * tile, tile), tile)] = p.astype(bf16)
        elif carry is not None:
            out_ref[...] = p + acc_ref[...]
        else:
            out_ref[...] = p

        if pool is not None:

            @pl.when(n == tiles - 1)
            def _():
                fetch.wait()
                low = dot_t(xs[...], held[...])
                if carry is not None:
                    low = low + sum_ref[...]
                if choose is None:
                    low_ref[...] = low
                else:
                    low = jnp.where(ids_ref[...] == owner_ref[...], low, 0.0)
                    chosen = low[:, :lanes]
                    for j in range(1, pool_rows // lanes):
                        chosen = chosen + low[:, j * lanes : (j + 1) * lanes]
                    out_ref[:, features:] = chosen.astype(bf16)

    in_specs = [constant(a.shape) for a in flat]
    operands = list(flat)
    for array, row, count in weights:
        if row % count == 0:
            spec = pl.BlockSpec((count, tile), lambda n, at=row // count: (at, n))
        else:
            spec = pl.BlockSpec(
                (pl.Element(count), pl.Element(tile)), lambda n, at=row: (at, n * tile)
            )
        in_specs.append(spec)
        operands.append(array)
    if pool is not None:
        in_specs.append(pl.BlockSpec(memory_space=pl.ANY))
        operands.append(pool)
    if choose is not None:
        owner, ids = choose
        in_specs += [constant((1, pool_rows)), constant((rows, 1))]
        operands += [owner, ids]
    if carry is not None:
        in_specs += [pl.BlockSpec((rows, tile), lambda n: (0, n)), constant((rows, pool_rows))]
        operands += list(carry)
    if choose is not None:
        out_shape = jax.ShapeDtypeStruct((rows, features + lanes), bf16)
        out_specs = pl.BlockSpec((rows, features + lanes), lambda n: (0, 0))
    else:
        out_shape = jax.ShapeDtypeStruct((rows, features), f32)
        out_specs = pl.BlockSpec((rows, tile), lambda n: (0, n))
        if pool is not None:
            out_shape = [out_shape, jax.ShapeDtypeStruct((rows, pool_rows), f32)]
            out_specs = [out_specs, pl.BlockSpec((rows, pool_rows), lambda n: (0, 0))]
    scratch = [pltpu.VMEM((rows, depth), bf16)]
    if pool is not None:
        scratch += [pltpu.VMEM((pool_rows, depth), bf16), pltpu.SemaphoreType.DMA(())]
    return pl.pallas_call(
        kernel,
        grid=(tiles,),
        in_specs=in_specs,
        out_specs=out_specs,
        out_shape=out_shape,
        scratch_shapes=scratch,
        compiler_params=pltpu.CompilerParams(vmem_limit_bytes=vmem),
        cost_estimate=pl.CostEstimate(flops=flops, bytes_accessed=1000, transcendentals=0),
        name="product" if choose is None else "product_sent",
    )(*operands)


def finish(acc, low, at, partial, part_at, pool, width, owner, ids, row, rows, prev):
    features = acc.shape[1]
    pool_rows = pool.shape[0]
    tile = 512
    tiles = features // tile

    def kernel(row_ref, *refs):
        refs = list(refs)
        acc_ref, low_ref, up_ref, owner_ref, ids_ref = [refs.pop(0) for _ in range(5)]
        if partial is not None:
            part_ref, sent_ref = refs.pop(0), refs.pop(0)
        if prev is not None:
            refs.pop(0)
        (out_ref,) = refs
        total = low_ref[...]
        y = acc_ref[...]
        if partial is not None:
            sent = sent_ref[...].astype(f32)
            total = total + jnp.concatenate([sent] * (pool_rows // lanes), axis=1)
            y = y + part_ref[...].astype(f32)
        mask = jnp.where(ids_ref[...] == owner_ref[...], total, 0.0).astype(bf16)
        y = y + adapter_scale * jnp.dot(mask, up_ref[...], preferred_element_type=f32)
        out_ref[...] = y.astype(bf16)

    in_specs = [
        pl.BlockSpec((rows, tile), lambda n, r: (at, n)),
        pl.BlockSpec((rows, pool_rows), lambda n, r: (at, 0)),
        pl.BlockSpec((pool_rows, tile), lambda n, r: (0, width // tile + n)),
        pl.BlockSpec((1, pool_rows), lambda n, r: (0, 0)),
        pl.BlockSpec((rows, 1), lambda n, r: (r[0], 0)),
    ]
    operands = [acc, low, pool, owner, ids]
    if partial is not None:
        in_specs += [
            pl.BlockSpec((rows, tile), lambda n, r: (part_at, n)),
            pl.BlockSpec((rows, lanes), lambda n, r: (part_at, features // lanes)),
        ]
        operands += [partial, partial]
    aliases = {}
    if prev is not None:
        in_specs.append(pl.BlockSpec(memory_space=pl.ANY))
        operands.append(prev)
        aliases = {len(operands): 0}
    return pl.pallas_call(
        kernel,
        grid_spec=pltpu.PrefetchScalarGridSpec(
            num_scalar_prefetch=1,
            grid=(tiles,),
            in_specs=in_specs,
            out_specs=pl.BlockSpec((rows, tile), lambda n, r: (r[0], n)),
        ),
        out_shape=jax.ShapeDtypeStruct((ids.shape[0], features), bf16),
        input_output_aliases=aliases,
        compiler_params=pltpu.CompilerParams(vmem_limit_bytes=vmem // 4),
        cost_estimate=pl.CostEstimate(flops=1000, bytes_accessed=1000, transcendentals=0),
        name="finish",
    )(row.reshape(1), *operands)


def body(
    layer_input,
    input_norm_weight,
    query_base_matrix,
    adapter_down_weight,
    adapter_up_weight,
    token_adapter_index,
):
    rows, width = layer_input.shape
    count = lax.axis_size("replica")
    rank = adapter_down_weight.shape[2]
    t = lax.axis_index("tensor").astype(jnp.int32)
    q = lax.axis_index("groups") * count + lax.axis_index("replica")
    inward = lambda a: lax.ppermute(a, "tensor", [(0, 1), (3, 2)])
    outward = lambda a: lax.ppermute(a, "tensor", [(1, 0), (2, 3)])
    cross = lambda a: lax.ppermute(a, "tensor", [(1, 2), (2, 1)])


    h = width * 7 // 16
    m = (width + h) // 2
    piece = h // (count * lax.axis_size("groups"))
    share = lax.dynamic_slice_in_dim(query_base_matrix, q * piece, piece, 0)
    sent = inward(share)
    layer_input = after(layer_input, share)
    adapter_down_weight = after(adapter_down_weight, share)
    pool = jnp.concatenate([adapter_down_weight[0].T, adapter_up_weight[0]], axis=1)
    pool = lax.all_gather(pool, "replica", axis=0, tiled=True)
    owner = jnp.repeat(jnp.arange(count, dtype=jnp.int32), rank)[None, :]
    ids = token_adapter_index[:, None]

    c = h + (width - h) * 7 // 9
    own_h, own_a, own_b, own_d0, own_d1 = norm_chunks(
        layer_input,
        input_norm_weight[None, :],
        [(0, h), (h, c), (c, width), (h, m), (m, width)],
    )
    w = [(query_base_matrix, 0, width)]
    own = product([(0, 0, [own_h]), (0, h, [own_a]), (0, c, [own_b])], rows, 0, w)
    out_own_a = outward(own_a)
    mid_a = cross(own_a)
    out_own_b = outward(after(own_b, out_own_a))
    mid_b = cross(after(own_b, mid_a))
    out_mid_a = outward(after(mid_a, out_own_a))
    end_d0 = inward(after(own_d0, sent))
    mid_h = cross(after(own_h, mid_a))
    out_mid_b = outward(after(mid_b, out_own_b))
    mid_row = jnp.where(t < 2, 2, 1).astype(jnp.int32)
    far_row = jnp.where(t < 2, 3, 0).astype(jnp.int32)
    last = (pool, width, owner, ids)
    own_low = (
        dot_t(own_h, pool[:, :h]) + dot_t(own_a, pool[:, h:c]) + dot_t(after(own_b, out_own_b, mid_b), pool[:, c:width])
    )
    out = finish(own, own_low, 0, None, 0, *last, t, rows, None)
    end_d1 = inward(after(own_d1, end_d0, out))
    far_d0 = cross(after(end_d0, mid_h))
    mid = product([(0, 0, [mid_h])], rows, 0, [(query_base_matrix, 0, h)], pool)
    end_h = inward(after(own_h, end_d1, out_mid_a, mid[0]))
    out_far0 = outward(after(far_d0, out_mid_b))
    far_d1 = cross(after(end_d1, far_d0))
    mid = product(
        [(0, h, [after(mid_a, far_d0), out_mid_a]), (0, c, [mid_b, out_mid_b])],
        rows, h, [(query_base_matrix, h, width - h)], pool, None, mid,
    )
    out_far1 = outward(after(far_d1, out_far0, mid[0]))
    far_h = cross(after(end_h, far_d1))
    sent = after(sent, mid_a, out_own_a, own)
    sent = lax.all_gather(sent, ("groups", "replica"), axis=0, tiled=True)
    help_weight = [(sent, 0, h)]

    pick = lambda row: lax.dynamic_slice_in_dim(ids, row * rows, rows, 0)
    ids_near = jnp.concatenate([pick(t), pick(mid_row)], axis=0)
    part_near = product(
        [(0, 0, [own_h]), (rows, 0, [mid_h])], 2 * rows, 0, help_weight, pool,
        (owner, ids_near),
    )
    distant = product(
        [
            (0, h, [after(end_d0, part_near), (out_own_a, 0, m - h)]),
            (0, m, [(end_d1, 0, c - m), (out_own_a, m - h, c - h)]),
            (0, c, [(end_d1, c - m, width - m), out_own_b]),
            (rows, h, [far_d0, out_far0]),
            (rows, m, [far_d1, out_far1]),
        ],
        2 * rows, h, [(query_base_matrix, h, width - h)], pool,
    )
    part_near = outward(after(part_near, out_far1))
    far_h = after(far_h, distant[0])
    part_far = product([(0, 0, [far_h])], rows, 0, help_weight, pool, (owner, pick(far_row)))
    far_h = after(far_h, part_far)
    part_far = outward(part_far)
    distant = product(
        [(0, 0, [end_h]), (rows, 0, [far_h])],
        2 * rows, 0, [(query_base_matrix, 0, h)], pool, None, distant,
    )
    out = finish(*mid, 0, part_near, 1, *last, mid_row, rows, out)
    out = finish(*distant, 0, part_near, 0, *last, t ^ 1, rows, out)
    return finish(*distant, 1, part_far, 0, *last, far_row, rows, out)


def solution(mesh):
    placed = (
        P(("groups", "replica", "tensor"), None),
        P(),
        P(None, "tensor"),
        P("replica", None, None),
        P("replica", None, "tensor"),
        P(("groups", "replica")),
    )
    line = mesh.shape["tensor"] == 4 and mesh.shape["replica"] == 4 and mesh.shape["groups"] == 2
    return jax.shard_map(
        body if line else plain,
        mesh=mesh,
        in_specs=placed,
        out_specs=P(("groups", "replica"), "tensor"),
        check_vma=False,
    )
```

```python
import jax
import jax.numpy as jnp
from jax import lax
from jax.experimental import pallas as pl
from jax.experimental.pallas import tpu as pltpu
from jax.sharding import PartitionSpec as P

adapter_scale = 2.0
lanes = 128
vmem = 56 * 1024 * 1024
f32 = jnp.float32
bf16 = jnp.bfloat16


def plain(
    layer_input,
    input_norm_weight,
    query_base_matrix,
    adapter_down_weight,
    adapter_up_weight,
    token_adapter_index,
):
    xf = layer_input.astype(f32)
    ms = jnp.mean(xf * xf, axis=-1, keepdims=True)
    normed = (xf * lax.rsqrt(ms + 1e-05) * input_norm_weight.astype(f32)).astype(bf16)
    gathered = lax.all_gather(normed, "tensor", axis=0, tiled=True)
    down_all = lax.all_gather(adapter_down_weight, "replica", axis=0, tiled=True)
    up_all = lax.all_gather(adapter_up_weight, "replica", axis=0, tiled=True)
    count, width, rank = down_all.shape
    down_cat = jnp.transpose(down_all, (1, 0, 2)).reshape(width, count * rank)
    low_all = jnp.dot(gathered, down_cat, preferred_element_type=f32)
    owner = jnp.repeat(jnp.arange(count, dtype=jnp.int32), rank)
    chosen = token_adapter_index[:, None] == owner[None, :]
    masked = jnp.where(chosen, low_all, 0.0).astype(bf16)
    update = jnp.dot(
        masked, up_all.reshape(count * rank, up_all.shape[2]), preferred_element_type=f32
    )
    base = jnp.dot(gathered, query_base_matrix, preferred_element_type=f32)
    return (base + adapter_scale * update).astype(bf16)


def norm_chunks(x, gain, spans):
    rows, width = x.shape
    block = 48

    def kernel(x_ref, g_ref, *out_refs):
        xf = x_ref[...].astype(f32)
        ms = jnp.mean(xf * xf, axis=-1, keepdims=True)
        y = (xf * lax.rsqrt(ms + 1e-05) * g_ref[...].astype(f32)).astype(bf16)
        for (lo, hi), out_ref in zip(spans, out_refs):
            out_ref[...] = y[:, lo:hi]

    return pl.pallas_call(
        kernel,
        grid=(rows // block,),
        in_specs=[
            pl.BlockSpec((block, width), lambda i: (i, 0)),
            pl.BlockSpec((1, width), lambda i: (0, 0)),
        ],
        out_specs=[pl.BlockSpec((block, hi - lo), lambda i: (i, 0)) for lo, hi in spans],
        out_shape=[jax.ShapeDtypeStruct((rows, hi - lo), bf16) for lo, hi in spans],
        compiler_params=pltpu.CompilerParams(vmem_limit_bytes=vmem // 2),
        cost_estimate=pl.CostEstimate(flops=1000, bytes_accessed=1000, transcendentals=0),
        name="norm_chunks",
    )(x, gain)


def dot_t(a, b):
    return lax.dot_general(a, b, (((1,), (1,)), ((), ())), preferred_element_type=f32)


def after(x, *others):
    return lax.optimization_barrier((x, *others))[0]


def constant(shape):
    return pl.BlockSpec(shape, lambda *_: (0, 0), pipeline_mode=pl.Buffered(1))


def product(pieces, rows, first, weights, pool=None, choose=None, carry=None, flops=1000):
    features = weights[0][0].shape[1]
    depth = sum(count for _, _, count in weights)
    pool_rows = 0 if pool is None else pool.shape[0]
    tile = 256
    tiles = features // tile
    whole = lambda a: a if isinstance(a, tuple) else (a, 0, a.shape[1])
    pieces = [(r, f, [whole(a) for a in arrays]) for r, f, arrays in pieces]
    flat = []
    for _, _, arrays in pieces:
        flat += [a for a, _, _ in arrays if not any(a is b for b in flat)]

    def kernel(*refs):
        refs = list(refs)
        take = lambda count: [refs.pop(0) for _ in range(count)]
        x_refs, w_refs = take(len(flat)), take(len(weights))
        if pool is not None:
            (down_ref,) = take(1)
        if choose is not None:
            owner_ref, ids_ref = take(2)
        if carry is not None:
            acc_ref, sum_ref = take(2)
        (out_ref,) = take(1)
        if pool is not None and choose is None:
            (low_ref,) = take(1)
        (xs,) = take(1)
        if pool is not None:
            held, sem = take(2)
            fetch = pltpu.make_async_copy(down_ref.at[:, pl.ds(first, depth)], held, sem)
        n = pl.program_id(0)

        @pl.when(n == 0)
        def _():
            for row, feature, arrays in pieces:
                x = None
                for a, lo, hi in arrays:
                    (at,) = [i for i, b in enumerate(flat) if a is b]
                    y = x_refs[at][:, lo:hi]
                    x = y if x is None else x + y
                at = feature - first
                xs[row : row + x.shape[0], at : at + x.shape[1]] = x
            if pool is not None:
                fetch.start()

        p = None
        at = 0
        for w_ref in w_refs:
            x = xs[:, at : at + w_ref.shape[0]]
            at += w_ref.shape[0]
            y = jnp.dot(x, w_ref[...], preferred_element_type=f32)
            p = y if p is None else p + y
        if choose is not None:
            out_ref[:, pl.ds(pl.multiple_of(n * tile, tile), tile)] = p.astype(bf16)
        elif carry is not None:
            out_ref[...] = p + acc_ref[...]
        else:
            out_ref[...] = p

        if pool is not None:

            @pl.when(n == tiles - 1)
            def _():
                fetch.wait()
                low = dot_t(xs[...], held[...])
                if carry is not None:
                    low = low + sum_ref[...]
                if choose is None:
                    low_ref[...] = low
                else:
                    low = jnp.where(ids_ref[...] == owner_ref[...], low, 0.0)
                    chosen = low[:, :lanes]
                    for j in range(1, pool_rows // lanes):
                        chosen = chosen + low[:, j * lanes : (j + 1) * lanes]
                    out_ref[:, features:] = chosen.astype(bf16)

    in_specs = [constant(a.shape) for a in flat]
    operands = list(flat)
    for array, row, count in weights:
        if row % count == 0:
            spec = pl.BlockSpec((count, tile), lambda n, at=row // count: (at, n))
        else:
            spec = pl.BlockSpec(
                (pl.Element(count), pl.Element(tile)), lambda n, at=row: (at, n * tile)
            )
        in_specs.append(spec)
        operands.append(array)
    if pool is not None:
        in_specs.append(pl.BlockSpec(memory_space=pl.ANY))
        operands.append(pool)
    if choose is not None:
        owner, ids = choose
        in_specs += [constant((1, pool_rows)), constant((rows, 1))]
        operands += [owner, ids]
    if carry is not None:
        in_specs += [pl.BlockSpec((rows, tile), lambda n: (0, n)), constant((rows, pool_rows))]
        operands += list(carry)
    if choose is not None:
        out_shape = jax.ShapeDtypeStruct((rows, features + lanes), bf16)
        out_specs = pl.BlockSpec((rows, features + lanes), lambda n: (0, 0))
    else:
        out_shape = jax.ShapeDtypeStruct((rows, features), f32)
        out_specs = pl.BlockSpec((rows, tile), lambda n: (0, n))
        if pool is not None:
            out_shape = [out_shape, jax.ShapeDtypeStruct((rows, pool_rows), f32)]
            out_specs = [out_specs, pl.BlockSpec((rows, pool_rows), lambda n: (0, 0))]
    scratch = [pltpu.VMEM((rows, depth), bf16)]
    if pool is not None:
        scratch += [pltpu.VMEM((pool_rows, depth), bf16), pltpu.SemaphoreType.DMA(())]
    return pl.pallas_call(
        kernel,
        grid=(tiles,),
        in_specs=in_specs,
        out_specs=out_specs,
        out_shape=out_shape,
        scratch_shapes=scratch,
        compiler_params=pltpu.CompilerParams(vmem_limit_bytes=vmem),
        cost_estimate=pl.CostEstimate(flops=flops, bytes_accessed=1000, transcendentals=0),
        name="product" if choose is None else "product_sent",
    )(*operands)


def finish(acc, low, at, partial, part_at, pool, width, owner, ids, row, rows, prev):
    features = acc.shape[1]
    pool_rows = pool.shape[0]
    tile = 512
    tiles = features // tile

    def kernel(row_ref, *refs):
        refs = list(refs)
        acc_ref, low_ref, up_ref, owner_ref, ids_ref = [refs.pop(0) for _ in range(5)]
        if partial is not None:
            part_ref, sent_ref = refs.pop(0), refs.pop(0)
        if prev is not None:
            refs.pop(0)
        (out_ref,) = refs
        total = low_ref[...]
        y = acc_ref[...]
        if partial is not None:
            sent = sent_ref[...].astype(f32)
            total = total + jnp.concatenate([sent] * (pool_rows // lanes), axis=1)
            y = y + part_ref[...].astype(f32)
        mask = jnp.where(ids_ref[...] == owner_ref[...], total, 0.0).astype(bf16)
        y = y + adapter_scale * jnp.dot(mask, up_ref[...], preferred_element_type=f32)
        out_ref[...] = y.astype(bf16)

    in_specs = [
        pl.BlockSpec((rows, tile), lambda n, r: (at, n)),
        pl.BlockSpec((rows, pool_rows), lambda n, r: (at, 0)),
        pl.BlockSpec((pool_rows, tile), lambda n, r: (0, width // tile + n)),
        pl.BlockSpec((1, pool_rows), lambda n, r: (0, 0)),
        pl.BlockSpec((rows, 1), lambda n, r: (r[0], 0)),
    ]
    operands = [acc, low, pool, owner, ids]
    if partial is not None:
        in_specs += [
            pl.BlockSpec((rows, tile), lambda n, r: (part_at, n)),
            pl.BlockSpec((rows, lanes), lambda n, r: (part_at, features // lanes)),
        ]
        operands += [partial, partial]
    aliases = {}
    if prev is not None:
        in_specs.append(pl.BlockSpec(memory_space=pl.ANY))
        operands.append(prev)
        aliases = {len(operands): 0}
    return pl.pallas_call(
        kernel,
        grid_spec=pltpu.PrefetchScalarGridSpec(
            num_scalar_prefetch=1,
            grid=(tiles,),
            in_specs=in_specs,
            out_specs=pl.BlockSpec((rows, tile), lambda n, r: (r[0], n)),
        ),
        out_shape=jax.ShapeDtypeStruct((ids.shape[0], features), bf16),
        input_output_aliases=aliases,
        compiler_params=pltpu.CompilerParams(vmem_limit_bytes=vmem // 4),
        cost_estimate=pl.CostEstimate(flops=1000, bytes_accessed=1000, transcendentals=0),
        name="finish",
    )(row.reshape(1), *operands)


def body(
    layer_input,
    input_norm_weight,
    query_base_matrix,
    adapter_down_weight,
    adapter_up_weight,
    token_adapter_index,
):
    rows, width = layer_input.shape
    count = lax.axis_size("replica")
    rank = adapter_down_weight.shape[2]
    t = lax.axis_index("tensor").astype(jnp.int32)
    q = lax.axis_index("groups") * count + lax.axis_index("replica")
    inward = lambda a: lax.ppermute(a, "tensor", [(0, 1), (3, 2)])
    outward = lambda a: lax.ppermute(a, "tensor", [(1, 0), (2, 3)])
    cross = lambda a: lax.ppermute(a, "tensor", [(1, 2), (2, 1)])


    h = width * 7 // 16
    m = (width + h) // 2
    piece = h // (count * lax.axis_size("groups"))
    share = lax.dynamic_slice_in_dim(query_base_matrix, q * piece, piece, 0)
    sent = inward(share)
    layer_input = after(layer_input, share)
    adapter_down_weight = after(adapter_down_weight, share)
    pool = jnp.concatenate([adapter_down_weight[0].T, adapter_up_weight[0]], axis=1)
    pool = lax.all_gather(pool, "replica", axis=0, tiled=True)
    owner = jnp.repeat(jnp.arange(count, dtype=jnp.int32), rank)[None, :]
    ids = token_adapter_index[:, None]

    c = h + (width - h) * 7 // 9
    own_h, own_a, own_b, own_d0, own_d1 = norm_chunks(
        layer_input,
        input_norm_weight[None, :],
        [(0, h), (h, c), (c, width), (h, m), (m, width)],
    )
    w = [(query_base_matrix, 0, width)]
    own = product([(0, 0, [own_h]), (0, h, [own_a]), (0, c, [own_b])], rows, 0, w)
    out_own_a = outward(own_a)
    mid_a = cross(own_a)
    out_own_b = outward(after(own_b, out_own_a))
    mid_b = cross(after(own_b, mid_a))
    out_mid_a = outward(after(mid_a, out_own_a))
    end_d0 = inward(after(own_d0, sent))
    mid_h = cross(after(own_h, mid_a))
    out_mid_b = outward(after(mid_b, out_own_b))
    mid_row = jnp.where(t < 2, 2, 1).astype(jnp.int32)
    far_row = jnp.where(t < 2, 3, 0).astype(jnp.int32)
    last = (pool, width, owner, ids)
    own_low = (
        dot_t(own_h, pool[:, :h]) + dot_t(own_a, pool[:, h:c]) + dot_t(after(own_b, out_own_b, mid_b), pool[:, c:width])
    )
    out = finish(own, own_low, 0, None, 0, *last, t, rows, None)
    end_d1 = inward(after(own_d1, end_d0, out))
    far_d0 = cross(after(end_d0, mid_h))
    mid = product([(0, 0, [mid_h])], rows, 0, [(query_base_matrix, 0, h)], pool)
    end_h = inward(after(own_h, end_d1, out_mid_a, mid[0]))
    out_far0 = outward(after(far_d0, out_mid_b))
    far_d1 = cross(after(end_d1, far_d0))
    mid = product(
        [(0, h, [after(mid_a, far_d0), out_mid_a]), (0, c, [mid_b, out_mid_b])],
        rows, h, [(query_base_matrix, h, width - h)], pool, None, mid,
    )
    out_far1 = outward(after(far_d1, out_far0, mid[0]))
    far_h = cross(after(end_h, far_d1))
    sent = after(sent, mid_a, out_own_a, own)
    sent = lax.all_gather(sent, ("groups", "replica"), axis=0, tiled=True)
    help_weight = [(sent, 0, h)]

    pick = lambda row: lax.dynamic_slice_in_dim(ids, row * rows, rows, 0)
    ids_near = jnp.concatenate([pick(t), pick(mid_row)], axis=0)
    part_near = product(
        [(0, 0, [own_h]), (rows, 0, [mid_h])], 2 * rows, 0, help_weight, pool,
        (owner, ids_near),
    )
    distant = product(
        [
            (0, h, [after(end_d0, part_near), (out_own_a, 0, m - h)]),
            (0, m, [(end_d1, 0, c - m), (out_own_a, m - h, c - h)]),
            (0, c, [(end_d1, c - m, width - m), out_own_b]),
            (rows, h, [far_d0, out_far0]),
            (rows, m, [far_d1, out_far1]),
        ],
        2 * rows, h, [(query_base_matrix, h, width - h)], pool,
    )
    part_near = outward(after(part_near, out_far1))
    far_h = after(far_h, distant[0])
    part_far = product([(0, 0, [far_h])], rows, 0, help_weight, pool, (owner, pick(far_row)))
    far_h = after(far_h, part_far)
    part_far = outward(part_far)
    distant = product(
        [(0, 0, [end_h]), (rows, 0, [far_h])],
        2 * rows, 0, [(query_base_matrix, 0, h)], pool, None, distant,
    )
    out = finish(*mid, 0, part_near, 1, *last, mid_row, rows, out)
    out = finish(*distant, 0, part_near, 0, *last, t ^ 1, rows, out)
    return finish(*distant, 1, part_far, 0, *last, far_row, rows, out)


def solution(mesh):
    placed = (
        P(("groups", "replica", "tensor"), None),
        P(),
        P(None, "tensor"),
        P("replica", None, None),
        P("replica", None, "tensor"),
        P(("groups", "replica")),
    )
    line = mesh.shape["tensor"] == 4 and mesh.shape["replica"] == 4 and mesh.shape["groups"] == 2
    return jax.shard_map(
        body if line else plain,
        mesh=mesh,
        in_specs=placed,
        out_specs=P(("groups", "replica"), "tensor"),
        check_vma=False,
    )
```

```python
import jax
import jax.numpy as jnp
from jax import lax
from jax.experimental import pallas as pl
from jax.experimental.pallas import tpu as pltpu
from jax.sharding import PartitionSpec as P

adapter_scale = 2.0
lanes = 128
vmem = 52 * 1024 * 1024
f32 = jnp.float32
bf16 = jnp.bfloat16


def plain(
    layer_input,
    input_norm_weight,
    query_base_matrix,
    adapter_down_weight,
    adapter_up_weight,
    token_adapter_index,
):
    xf = layer_input.astype(f32)
    ms = jnp.mean(xf * xf, axis=-1, keepdims=True)
    normed = (xf * lax.rsqrt(ms + 1e-05) * input_norm_weight.astype(f32)).astype(bf16)
    gathered = lax.all_gather(normed, "tensor", axis=0, tiled=True)
    down_all = lax.all_gather(adapter_down_weight, "replica", axis=0, tiled=True)
    up_all = lax.all_gather(adapter_up_weight, "replica", axis=0, tiled=True)
    count, width, rank = down_all.shape
    down_cat = jnp.transpose(down_all, (1, 0, 2)).reshape(width, count * rank)
    low_all = jnp.dot(gathered, down_cat, preferred_element_type=f32)
    owner = jnp.repeat(jnp.arange(count, dtype=jnp.int32), rank)
    chosen = token_adapter_index[:, None] == owner[None, :]
    masked = jnp.where(chosen, low_all, 0.0).astype(bf16)
    update = jnp.dot(
        masked, up_all.reshape(count * rank, up_all.shape[2]), preferred_element_type=f32
    )
    base = jnp.dot(gathered, query_base_matrix, preferred_element_type=f32)
    return (base + adapter_scale * update).astype(bf16)


def norm_chunks(x, gain, spans):
    rows, width = x.shape
    block = 48

    def kernel(x_ref, g_ref, *out_refs):
        xf = x_ref[...].astype(f32)
        ms = jnp.mean(xf * xf, axis=-1, keepdims=True)
        y = (xf * lax.rsqrt(ms + 1e-05) * g_ref[...].astype(f32)).astype(bf16)
        for (lo, hi), out_ref in zip(spans, out_refs):
            out_ref[...] = y[:, lo:hi]

    return pl.pallas_call(
        kernel,
        grid=(rows // block,),
        in_specs=[
            pl.BlockSpec((block, width), lambda i: (i, 0)),
            pl.BlockSpec((1, width), lambda i: (0, 0)),
        ],
        out_specs=[pl.BlockSpec((block, hi - lo), lambda i: (i, 0)) for lo, hi in spans],
        out_shape=[jax.ShapeDtypeStruct((rows, hi - lo), bf16) for lo, hi in spans],
        compiler_params=pltpu.CompilerParams(vmem_limit_bytes=vmem // 2),
        cost_estimate=pl.CostEstimate(flops=1000, bytes_accessed=1000, transcendentals=0),
        name="norm_chunks",
    )(x, gain)


def dot_t(a, b):
    return lax.dot_general(a, b, (((1,), (1,)), ((), ())), preferred_element_type=f32)


def after(x, *others):
    return lax.optimization_barrier((x, *others))[0]


def constant(shape):
    return pl.BlockSpec(shape, lambda *_: (0, 0), pipeline_mode=pl.Buffered(1))


def product(pieces, rows, first, weights, pool=None, choose=None, carry=None, flops=1000):
    features = weights[0][0].shape[1]
    depth = sum(count for _, _, count in weights)
    pool_rows = 0 if pool is None else pool.shape[0]
    tile = 256
    tiles = features // tile
    whole = lambda a: a if isinstance(a, tuple) else (a, 0, a.shape[1])
    pieces = [(r, f, [whole(a) for a in arrays]) for r, f, arrays in pieces]
    flat = []
    for _, _, arrays in pieces:
        flat += [a for a, _, _ in arrays if not any(a is b for b in flat)]

    def kernel(*refs):
        refs = list(refs)
        take = lambda count: [refs.pop(0) for _ in range(count)]
        x_refs, w_refs = take(len(flat)), take(len(weights))
        if pool is not None:
            (down_ref,) = take(1)
        if choose is not None:
            owner_ref, ids_ref = take(2)
        if carry is not None:
            acc_ref, sum_ref = take(2)
        (out_ref,) = take(1)
        if pool is not None and choose is None:
            (low_ref,) = take(1)
        (xs,) = take(1)
        if pool is not None:
            held, sem = take(2)
            fetch = pltpu.make_async_copy(down_ref.at[:, pl.ds(first, depth)], held, sem)
        n = pl.program_id(0)

        @pl.when(n == 0)
        def _():
            for row, feature, arrays in pieces:
                x = None
                for a, lo, hi in arrays:
                    (at,) = [i for i, b in enumerate(flat) if a is b]
                    y = x_refs[at][:, lo:hi]
                    x = y if x is None else x + y
                at = feature - first
                xs[row : row + x.shape[0], at : at + x.shape[1]] = x
            if pool is not None:
                fetch.start()

        p = None
        at = 0
        for w_ref in w_refs:
            x = xs[:, at : at + w_ref.shape[0]]
            at += w_ref.shape[0]
            y = jnp.dot(x, w_ref[...], preferred_element_type=f32)
            p = y if p is None else p + y
        if choose is not None:
            out_ref[:, pl.ds(pl.multiple_of(n * tile, tile), tile)] = p.astype(bf16)
        elif carry is not None:
            out_ref[...] = p + acc_ref[...]
        else:
            out_ref[...] = p

        if pool is not None:

            @pl.when(n == tiles - 1)
            def _():
                fetch.wait()
                low = dot_t(xs[...], held[...])
                if carry is not None:
                    low = low + sum_ref[...]
                if choose is None:
                    low_ref[...] = low
                else:
                    low = jnp.where(ids_ref[...] == owner_ref[...], low, 0.0)
                    chosen = low[:, :lanes]
                    for j in range(1, pool_rows // lanes):
                        chosen = chosen + low[:, j * lanes : (j + 1) * lanes]
                    out_ref[:, features:] = chosen.astype(bf16)

    in_specs = [constant(a.shape) for a in flat]
    operands = list(flat)
    for array, row, count in weights:
        if row % count == 0:
            spec = pl.BlockSpec((count, tile), lambda n, at=row // count: (at, n))
        else:
            spec = pl.BlockSpec(
                (pl.Element(count), pl.Element(tile)), lambda n, at=row: (at, n * tile)
            )
        in_specs.append(spec)
        operands.append(array)
    if pool is not None:
        in_specs.append(pl.BlockSpec(memory_space=pl.ANY))
        operands.append(pool)
    if choose is not None:
        owner, ids = choose
        in_specs += [constant((1, pool_rows)), constant((rows, 1))]
        operands += [owner, ids]
    if carry is not None:
        in_specs += [pl.BlockSpec((rows, tile), lambda n: (0, n)), constant((rows, pool_rows))]
        operands += list(carry)
    if choose is not None:
        out_shape = jax.ShapeDtypeStruct((rows, features + lanes), bf16)
        out_specs = pl.BlockSpec((rows, features + lanes), lambda n: (0, 0))
    else:
        out_shape = jax.ShapeDtypeStruct((rows, features), f32)
        out_specs = pl.BlockSpec((rows, tile), lambda n: (0, n))
        if pool is not None:
            out_shape = [out_shape, jax.ShapeDtypeStruct((rows, pool_rows), f32)]
            out_specs = [out_specs, pl.BlockSpec((rows, pool_rows), lambda n: (0, 0))]
    scratch = [pltpu.VMEM((rows, depth), bf16)]
    if pool is not None:
        scratch += [pltpu.VMEM((pool_rows, depth), bf16), pltpu.SemaphoreType.DMA(())]
    return pl.pallas_call(
        kernel,
        grid=(tiles,),
        in_specs=in_specs,
        out_specs=out_specs,
        out_shape=out_shape,
        scratch_shapes=scratch,
        compiler_params=pltpu.CompilerParams(vmem_limit_bytes=vmem),
        cost_estimate=pl.CostEstimate(flops=flops, bytes_accessed=1000, transcendentals=0),
        name="product" if choose is None else "product_sent",
    )(*operands)


def finish(acc, low, at, partial, part_at, pool, width, owner, ids, row, rows, prev):
    features = acc.shape[1]
    pool_rows = pool.shape[0]
    tile = 512
    tiles = features // tile

    def kernel(row_ref, *refs):
        refs = list(refs)
        acc_ref, low_ref, up_ref, owner_ref, ids_ref = [refs.pop(0) for _ in range(5)]
        if partial is not None:
            part_ref, sent_ref = refs.pop(0), refs.pop(0)
        if prev is not None:
            refs.pop(0)
        (out_ref,) = refs
        total = low_ref[...]
        y = acc_ref[...]
        if partial is not None:
            sent = sent_ref[...].astype(f32)
            total = total + jnp.concatenate([sent] * (pool_rows // lanes), axis=1)
            y = y + part_ref[...].astype(f32)
        mask = jnp.where(ids_ref[...] == owner_ref[...], total, 0.0).astype(bf16)
        y = y + adapter_scale * jnp.dot(mask, up_ref[...], preferred_element_type=f32)
        out_ref[...] = y.astype(bf16)

    in_specs = [
        pl.BlockSpec((rows, tile), lambda n, r: (at, n)),
        pl.BlockSpec((rows, pool_rows), lambda n, r: (at, 0)),
        pl.BlockSpec((pool_rows, tile), lambda n, r: (0, width // tile + n)),
        pl.BlockSpec((1, pool_rows), lambda n, r: (0, 0)),
        pl.BlockSpec((rows, 1), lambda n, r: (r[0], 0)),
    ]
    operands = [acc, low, pool, owner, ids]
    if partial is not None:
        in_specs += [
            pl.BlockSpec((rows, tile), lambda n, r: (part_at, n)),
            pl.BlockSpec((rows, lanes), lambda n, r: (part_at, features // lanes)),
        ]
        operands += [partial, partial]
    aliases = {}
    if prev is not None:
        in_specs.append(pl.BlockSpec(memory_space=pl.ANY))
        operands.append(prev)
        aliases = {len(operands): 0}
    return pl.pallas_call(
        kernel,
        grid_spec=pltpu.PrefetchScalarGridSpec(
            num_scalar_prefetch=1,
            grid=(tiles,),
            in_specs=in_specs,
            out_specs=pl.BlockSpec((rows, tile), lambda n, r: (r[0], n)),
        ),
        out_shape=jax.ShapeDtypeStruct((ids.shape[0], features), bf16),
        input_output_aliases=aliases,
        compiler_params=pltpu.CompilerParams(vmem_limit_bytes=vmem // 4),
        cost_estimate=pl.CostEstimate(flops=1000, bytes_accessed=1000, transcendentals=0),
        name="finish",
    )(row.reshape(1), *operands)


def body(
    layer_input,
    input_norm_weight,
    query_base_matrix,
    adapter_down_weight,
    adapter_up_weight,
    token_adapter_index,
):
    rows, width = layer_input.shape
    count = lax.axis_size("replica")
    rank = adapter_down_weight.shape[2]
    t = lax.axis_index("tensor").astype(jnp.int32)
    q = lax.axis_index("groups") * count + lax.axis_index("replica")
    inward = lambda a: lax.ppermute(a, "tensor", [(0, 1), (3, 2)])
    outward = lambda a: lax.ppermute(a, "tensor", [(1, 0), (2, 3)])
    cross = lambda a: lax.ppermute(a, "tensor", [(1, 2), (2, 1)])


    h = width * 7 // 16
    m = (width + h) // 2
    piece = h // (count * lax.axis_size("groups"))
    share = lax.dynamic_slice_in_dim(query_base_matrix, q * piece, piece, 0)
    sent = inward(share)
    layer_input = after(layer_input, share)
    adapter_down_weight = after(adapter_down_weight, share)
    pool = jnp.concatenate([adapter_down_weight[0].T, adapter_up_weight[0]], axis=1)
    pool = lax.all_gather(pool, "replica", axis=0, tiled=True)
    owner = jnp.repeat(jnp.arange(count, dtype=jnp.int32), rank)[None, :]
    ids = token_adapter_index[:, None]

    c = h + (width - h) * 7 // 9
    own_h, own_a, own_b, own_d0, own_d1 = norm_chunks(
        layer_input,
        input_norm_weight[None, :],
        [(0, h), (h, c), (c, width), (h, m), (m, width)],
    )
    w = [(query_base_matrix, 0, width)]
    own = product([(0, 0, [own_h]), (0, h, [own_a]), (0, c, [own_b])], rows, 0, w)
    out_own_a = outward(own_a)
    mid_a = cross(own_a)
    out_own_b = outward(after(own_b, out_own_a))
    mid_b = cross(after(own_b, mid_a))
    out_mid_a = outward(after(mid_a, out_own_a))
    end_d0 = inward(after(own_d0, sent))
    mid_h = cross(after(own_h, mid_a))
    out_mid_b = outward(after(mid_b, out_own_b))
    mid_row = jnp.where(t < 2, 2, 1).astype(jnp.int32)
    far_row = jnp.where(t < 2, 3, 0).astype(jnp.int32)
    last = (pool, width, owner, ids)
    own_low = (
        dot_t(own_h, pool[:, :h]) + dot_t(own_a, pool[:, h:c]) + dot_t(after(own_b, out_own_b, mid_b), pool[:, c:width])
    )
    out = finish(own, own_low, 0, None, 0, *last, t, rows, None)
    end_d1 = inward(after(own_d1, end_d0, out))
    far_d0 = cross(after(end_d0, mid_h))
    mid = product([(0, 0, [mid_h])], rows, 0, [(query_base_matrix, 0, h)], pool)
    end_h = inward(after(own_h, end_d1, out_mid_a, mid[0]))
    out_far0 = outward(after(far_d0, out_mid_b))
    far_d1 = cross(after(end_d1, far_d0))
    mid = product(
        [(0, h, [after(mid_a, far_d0), out_mid_a]), (0, c, [mid_b, out_mid_b])],
        rows, h, [(query_base_matrix, h, width - h)], pool, None, mid,
    )
    out_far1 = outward(after(far_d1, out_far0, mid[0]))
    far_h = cross(after(end_h, far_d1))
    sent = after(sent, mid_a, out_own_a, own)
    sent = lax.all_gather(sent, ("groups", "replica"), axis=0, tiled=True)
    help_weight = [(sent, 0, h)]

    pick = lambda row: lax.dynamic_slice_in_dim(ids, row * rows, rows, 0)
    ids_near = jnp.concatenate([pick(t), pick(mid_row)], axis=0)
    part_near = product(
        [(0, 0, [own_h]), (rows, 0, [mid_h])], 2 * rows, 0, help_weight, pool,
        (owner, ids_near),
    )
    distant = product(
        [
            (0, h, [after(end_d0, part_near), (out_own_a, 0, m - h)]),
            (0, m, [(end_d1, 0, c - m), (out_own_a, m - h, c - h)]),
            (0, c, [(end_d1, c - m, width - m), out_own_b]),
            (rows, h, [far_d0, out_far0]),
            (rows, m, [far_d1, out_far1]),
        ],
        2 * rows, h, [(query_base_matrix, h, width - h)], pool,
    )
    part_near = outward(after(part_near, out_far1))
    far_h = after(far_h, distant[0])
    part_far = product([(0, 0, [far_h])], rows, 0, help_weight, pool, (owner, pick(far_row)))
    far_h = after(far_h, part_far)
    part_far = outward(part_far)
    distant = product(
        [(0, 0, [end_h]), (rows, 0, [far_h])],
        2 * rows, 0, [(query_base_matrix, 0, h)], pool, None, distant,
    )
    out = finish(*mid, 0, part_near, 1, *last, mid_row, rows, out)
    out = finish(*distant, 0, part_near, 0, *last, t ^ 1, rows, out)
    return finish(*distant, 1, part_far, 0, *last, far_row, rows, out)


def solution(mesh):
    placed = (
        P(("groups", "replica", "tensor"), None),
        P(),
        P(None, "tensor"),
        P("replica", None, None),
        P("replica", None, "tensor"),
        P(("groups", "replica")),
    )
    line = mesh.shape["tensor"] == 4 and mesh.shape["replica"] == 4 and mesh.shape["groups"] == 2
    return jax.shard_map(
        body if line else plain,
        mesh=mesh,
        in_specs=placed,
        out_specs=P(("groups", "replica"), "tensor"),
        check_vma=False,
    )
```
